32 devices in a mesh: wide: 8 (over z, x), narrow: 4 (over y, core).
Axes of the slice: x: 2, y: 2, z: 4, core: 2. Of those that a mesh axis runs over, the one named last changes fastest.
Arguments:
- tokens: bfloat16 [64, 320, 1152], P('wide', 'narrow'), may hold values from -6 to 6
- skip_store: bfloat16 [64, 320, 1152], P('wide', None, 'narrow'), may hold values from -6 to 6
- cotangent: bfloat16 [64, 320, 1152], P('wide', 'narrow'), may hold values from -6 to 6
- lengths: int32 [64], P('wide'), may hold values from 192 to 320, as said below
- w_skip: float32 [2304, 1152], P(('wide', 'narrow')), may hold values from -20 to 20
- mom_skip: float32 [2304, 1152], P(('wide', 'narrow')), may hold values from -572.4334 to 572.4334
- sq_skip: float32 [2304, 1152], P(('wide', 'narrow')), may hold values from 0 to 81920
- w_qkv: float32 [1152, 3456], P(('wide', 'narrow')), may hold values from -20 to 20
- mom_qkv: float32 [1152, 3456], P(('wide', 'narrow')), may hold values from -572.4334 to 572.4334
- sq_qkv: float32 [1152, 3456], P(('wide', 'narrow')), may hold values from 0 to 81920
- w_proj: float32 [1152, 1152], P(('wide', 'narrow')), may hold values from -20 to 20
- mom_proj: float32 [1152, 1152], P(('wide', 'narrow')), may hold values from -572.4334 to 572.4334
- sq_proj: float32 [1152, 1152], P(('wide', 'narrow')), may hold values from 0 to 81920
- w_fc1: float32 [1152, 4608], P(('wide', 'narrow')), may hold values from -20 to 20
- mom_fc1: float32 [1152, 4608], P(('wide', 'narrow')), may hold values from -572.4334 to 572.4334
- sq_fc1: float32 [1152, 4608], P(('wide', 'narrow')), may hold values from 0 to 81920
- w_fc2: float32 [4608, 1152], P(('wide', 'narrow')), may hold values from -20 to 20
- mom_fc2: float32 [4608, 1152], P(('wide', 'narrow')), may hold values from -572.4334 to 572.4334
- sq_fc2: float32 [4608, 1152], P(('wide', 'narrow')), may hold values from 0 to 81920
- norm_table: float32 [1152, 4], P(('wide', 'narrow')), may hold values from -2 to 2
- norm_mom: float32 [1152, 4], P(('wide', 'narrow')), may hold values from -715.54175 to 715.54175
- norm_sq: float32 [1152, 4], P(('wide', 'narrow')), may hold values from 0 to 245760
Outputs:
- block_out: bfloat16 [64, 320, 1152], P('wide', 'narrow')
- grad_tokens: bfloat16 [64, 320, 1152], P('wide', 'narrow')
- grad_skip: bfloat16 [64, 320, 1152], P('wide', None, 'narrow')
- new_w_skip: float32 [2304, 1152], P(('wide', 'narrow'))
- new_mom_skip: float32 [2304, 1152], P(('wide', 'narrow'))
- new_sq_skip: float32 [2304, 1152], P(('wide', 'narrow'))
- copy_skip: bfloat16 [2304, 1152], P(('wide', 'narrow'))
- new_w_qkv: float32 [1152, 3456], P(('wide', 'narrow'))
- new_mom_qkv: float32 [1152, 3456], P(('wide', 'narrow'))
- new_sq_qkv: float32 [1152, 3456], P(('wide', 'narrow'))
- copy_qkv: bfloat16 [1152, 3456], P(('wide', 'narrow'))
- new_w_proj: float32 [1152, 1152], P(('wide', 'narrow'))
- new_mom_proj: float32 [1152, 1152], P(('wide', 'narrow'))
- new_sq_proj: float32 [1152, 1152], P(('wide', 'narrow'))
- copy_proj: bfloat16 [1152, 1152], P(('wide', 'narrow'))
- new_w_fc1: float32 [1152, 4608], P(('wide', 'narrow'))
- new_mom_fc1: float32 [1152, 4608], P(('wide', 'narrow'))
- new_sq_fc1: float32 [1152, 4608], P(('wide', 'narrow'))
- copy_fc1: bfloat16 [1152, 4608], P(('wide', 'narrow'))
- new_w_fc2: float32 [4608, 1152], P(('wide', 'narrow'))
- new_mom_fc2: float32 [4608, 1152], P(('wide', 'narrow'))
- new_sq_fc2: float32 [4608, 1152], P(('wide', 'narrow'))
- copy_fc2: bfloat16 [4608, 1152], P(('wide', 'narrow'))
- new_norm_table: float32 [1152, 4], P(('wide', 'narrow'))
- new_norm_mom: float32 [1152, 4], P(('wide', 'narrow'))
- new_norm_sq: float32 [1152, 4], P(('wide', 'narrow'))
- lamb_stats: float32 [3, 5], replicated
The draws below stay inside these ranges and needn't reach their ends.
Inputs may be any that keep to these rules, and one draw needn't show every extreme that they name: `lengths`: among the 8 items of each index of wide, one has length 320.
All inputs are finite; a program needn't handle non-finite values.
Results may differ from the reference program's by a relative error of at most 0.015.
The reference program's roundings to bfloat16 on the way count: a program that leaves them out, or rounds other values in their place, can miss the bound.
Values may be sent and summed in bfloat16 or wider, within the bound.
No kernel may reach another device: no remote copies, remote signals or barrier semaphores. Data moves between devices by JAX's collectives and lax.ppermute only.
A program may use at most 384 MiB of HBM per device.

```python
import math
import jax
import jax.numpy as jnp
from jax import lax

D = 1152
HEAD_DIM = 72
FF = 4608
ITEMS_DEV = 8
SLOT = 320
MIN_LEN = 192
STEP = 10
ITEMS = 64


def unit_entries(key, shape):
    key_normal = jax.random.fold_in(key, 0)
    normal = jnp.clip(jax.random.normal(key_normal, shape, jnp.float32), -4.0, 4.0)
    return normal


def spread_rows(key, rows, cols, fan_in, rise):
    key_base, key_jitter = jax.random.split(key)
    base = unit_entries(key_base, (rows, cols))
    place = jnp.arange(rows, dtype=jnp.float32) / max(rows - 1, 1)
    trend = jnp.exp(math.log(rise) * (place - 0.5))
    jitter = jnp.exp(jax.random.uniform(key_jitter, (rows,), jnp.float32, -1.15, 1.15))
    power = (rise - 1.0 / rise) / (2.0 * math.log(rise)) * (math.sinh(2.3) / 2.3)
    return base * (trend * jitter)[:, None] / math.sqrt(fan_in * power)


def grad_size(share):
    return share * math.sqrt(ITEMS * SLOT)


def first_moment(key, rows, cols, scale):
    return scale * jnp.clip(jax.random.normal(key, (rows, cols), jnp.float32), -4.0, 4.0)


def second_moment(key, rows, cols, scale):
    place = jnp.arange(rows, dtype=jnp.float32) / max(rows - 1, 1)
    fall = jnp.exp(math.log(4.0) * (1.0 - place))
    jitter = jnp.exp(jax.random.uniform(key, (rows, cols), jnp.float32, math.log(0.5), math.log(2.0)))
    return scale * scale * fall[:, None] * jitter


def draw_lengths(key, part):
    key = jax.random.fold_in(key, 301)
    key_base, key_pick = jax.random.split(key)
    groups = ITEMS // ITEMS_DEV
    base = jax.random.randint(key_base, (groups, ITEMS_DEV), MIN_LEN, SLOT + 1)
    chosen = jax.random.randint(key_pick, (groups, 1), 0, ITEMS_DEV)
    full = jnp.arange(ITEMS_DEV, dtype=jnp.int32)[None, :] == chosen
    return jnp.where(full, SLOT, base).reshape(ITEMS).astype(jnp.int32)


def draw_w_skip(key, part):
    key = jax.random.fold_in(key, 11)
    return spread_rows(key, 2 * D, D, 2 * D, 3.0)


def draw_w_qkv(key, part):
    key = jax.random.fold_in(key, 12)
    return spread_rows(key, D, 3 * D, D, 3.0)


def draw_w_proj(key, part):
    key = jax.random.fold_in(key, 13)
    return spread_rows(key, D, D, D // 64, 3.0)


def draw_w_fc1(key, part):
    key = jax.random.fold_in(key, 14)
    return spread_rows(key, D, FF, D, 3.0)


def draw_w_fc2(key, part):
    key = jax.random.fold_in(key, 15)
    return spread_rows(key, FF, D, FF // 2, 3.0)


def draw_mom_skip(key, part):
    key = jax.random.fold_in(key, 21)
    return first_moment(key, 2 * D, D, grad_size(0.7))


def draw_mom_qkv(key, part):
    key = jax.random.fold_in(key, 22)
    return first_moment(key, D, 3 * D, grad_size(0.2))


def draw_mom_proj(key, part):
    key = jax.random.fold_in(key, 23)
    return first_moment(key, D, D, grad_size(0.3))


def draw_mom_fc1(key, part):
    key = jax.random.fold_in(key, 24)
    return first_moment(key, D, FF, grad_size(0.3))


def draw_mom_fc2(key, part):
    key = jax.random.fold_in(key, 25)
    return first_moment(key, FF, D, grad_size(0.5))


def draw_sq_skip(key, part):
    key = jax.random.fold_in(key, 31)
    return second_moment(key, 2 * D, D, grad_size(0.7))


def draw_sq_qkv(key, part):
    key = jax.random.fold_in(key, 32)
    return second_moment(key, D, 3 * D, grad_size(0.2))


def draw_sq_proj(key, part):
    key = jax.random.fold_in(key, 33)
    return second_moment(key, D, D, grad_size(0.3))


def draw_sq_fc1(key, part):
    key = jax.random.fold_in(key, 34)
    return second_moment(key, D, FF, grad_size(0.3))


def draw_sq_fc2(key, part):
    key = jax.random.fold_in(key, 35)
    return second_moment(key, FF, D, grad_size(0.5))


def draw_norm_table(key, part):
    key = jax.random.fold_in(key, 41)
    key_gain, key_shift = jax.random.split(key)
    gain_part = 1.0 + 0.1 * unit_entries(key_gain, (D, 2))
    shift_part = 0.3 * unit_entries(key_shift, (D, 2))
    return jnp.stack([gain_part[:, 0], shift_part[:, 0], gain_part[:, 1], shift_part[:, 1]], 1)


def draw_norm_mom(key, part):
    key = jax.random.fold_in(key, 42)
    return first_moment(key, D, 4, grad_size(1.2))


def draw_norm_sq(key, part):
    key = jax.random.fold_in(key, 43)
    return second_moment(key, D, 4, grad_size(1.2))


def levels(own_key, extent, cuts, least, high):
    factor_of, own = 1.0, jax.random.fold_in(own_key, 6)
    for axis_at, shards_of in cuts:
        draws = jnp.exp(jax.random.uniform(jax.random.fold_in(own, axis_at), (shards_of,), jnp.float32, least / len(cuts), high / len(cuts)))
        factor_of = factor_of * jnp.repeat(draws, extent[axis_at] // shards_of).reshape([-1 if axis == axis_at else 1 for axis in range(len(extent))])
    return factor_of


def scatter_about(rng, dims, spread, limit, cuts=(), kind=jnp.bfloat16):
    drawn = spread * jax.random.normal(rng, dims, jnp.float32)
    if cuts:
        drawn = drawn * levels(rng, dims, cuts, -0.22, 0.18)
    return jnp.clip(drawn, -limit, limit).astype(kind)


def setup_inputs(seed: int = 0) -> dict:
    keys = jax.random.split(jax.random.key(seed), 23)
    tokens = scatter_about(keys[0], (ITEMS, SLOT, D), 1.0, 6.0, ((0, 8), (1, 4)))
    skip_store = scatter_about(keys[1], (ITEMS, SLOT, D), 1.0, 6.0, ((0, 8), (2, 4)))
    cotangent = scatter_about(keys[2], (ITEMS, SLOT, D), 1.0, 6.0, ((0, 8), (1, 4)))
    lengths = draw_lengths(jax.random.fold_in(keys[22], 71), 0)
    w_skip = draw_w_skip(jax.random.fold_in(keys[22], 71), 0)
    mom_skip = draw_mom_skip(jax.random.fold_in(keys[22], 71), 0)
    sq_skip = draw_sq_skip(jax.random.fold_in(keys[22], 71), 0)
    w_qkv = draw_w_qkv(jax.random.fold_in(keys[22], 71), 0)
    mom_qkv = draw_mom_qkv(jax.random.fold_in(keys[22], 71), 0)
    sq_qkv = draw_sq_qkv(jax.random.fold_in(keys[22], 71), 0)
    w_proj = draw_w_proj(jax.random.fold_in(keys[22], 71), 0)
    mom_proj = draw_mom_proj(jax.random.fold_in(keys[22], 71), 0)
    sq_proj = draw_sq_proj(jax.random.fold_in(keys[22], 71), 0)
    w_fc1 = draw_w_fc1(jax.random.fold_in(keys[22], 71), 0)
    mom_fc1 = draw_mom_fc1(jax.random.fold_in(keys[22], 71), 0)
    sq_fc1 = draw_sq_fc1(jax.random.fold_in(keys[22], 71), 0)
    w_fc2 = draw_w_fc2(jax.random.fold_in(keys[22], 71), 0)
    mom_fc2 = draw_mom_fc2(jax.random.fold_in(keys[22], 71), 0)
    sq_fc2 = draw_sq_fc2(jax.random.fold_in(keys[22], 71), 0)
    norm_table = draw_norm_table(jax.random.fold_in(keys[22], 71), 0)
    norm_mom = draw_norm_mom(jax.random.fold_in(keys[22], 71), 0)
    norm_sq = draw_norm_sq(jax.random.fold_in(keys[22], 71), 0)
    return dict(tokens=tokens, skip_store=skip_store, cotangent=cotangent, lengths=lengths, w_skip=w_skip, mom_skip=mom_skip, sq_skip=sq_skip, w_qkv=w_qkv, mom_qkv=mom_qkv, sq_qkv=sq_qkv, w_proj=w_proj, mom_proj=mom_proj, sq_proj=sq_proj, w_fc1=w_fc1, mom_fc1=mom_fc1, sq_fc1=sq_fc1, w_fc2=w_fc2, mom_fc2=mom_fc2, sq_fc2=sq_fc2, norm_table=norm_table, norm_mom=norm_mom, norm_sq=norm_sq)


@jax.custom_vjp
def low(v):
    return lax.optimization_barrier(v.astype(jnp.bfloat16)).astype(jnp.float32)

@jax.custom_vjp
def low_back(v):
    return v

def low_keep(v):
    return (low(v), None)

def low_pass(kept, grad):
    return (grad,)

def back_keep(v):
    return (v, None)

def back_low(kept, grad):
    return (low(grad),)
low.defvjp(low_keep, low_pass)
low_back.defvjp(back_keep, back_low)
EPS_NORM = 1e-05
BETA_ONE = 0.5
BETA_TWO = 0.5
EPS_ADAM = 1e-06
DECAY = 0.01
RATE = 0.5
RATE_TABLE = 0.1
NEGATIVE = -1e+30
HIGH = lax.Precision.HIGHEST

def multiply(left, right):
    return jnp.dot(left, right, precision=HIGH, preferred_element_type=jnp.float32)

def layer_norm(values, gain_col, shift_col):
    center = values - lax.optimization_barrier(jnp.mean(values, -1, keepdims=True))
    inv_std = lax.rsqrt(lax.optimization_barrier(jnp.mean(center * center, -1, keepdims=True)) + EPS_NORM)
    return center * inv_std * gain_col + shift_col

def attend(queries, key_rows, value_rows, key_valid):
    raw = jnp.einsum('inhd,imhd->ihnm', queries, key_rows, precision=HIGH)
    logits = low_back(raw * (1.0 / math.sqrt(HEAD_DIM)))
    logits = jnp.where(key_valid[:, None, None, :], logits, NEGATIVE)
    shifted = logits - lax.optimization_barrier(jnp.max(logits, -1, keepdims=True))
    expo = jnp.exp(shifted)
    attn_probs = low(expo / lax.optimization_barrier(jnp.sum(expo, -1, keepdims=True)))
    return jnp.einsum('ihnm,imhd->inhd', attn_probs, value_rows, precision=HIGH)

def block(params, token_rows, skip_rows, key_valid):
    w_skip, w_qkv, w_proj, w_fc1, w_fc2, table = [low(param) for param in params]
    item_count, row_count, model_width = token_rows.shape
    row_total = item_count * row_count
    joined = jnp.concatenate([token_rows, skip_rows], -1).reshape(row_total, 2 * model_width)
    first = low_back(multiply(joined, w_skip))
    act_one = low(layer_norm(first, table[:, 0], table[:, 1]))
    projected = low(low_back(multiply(act_one, w_qkv)))
    queries = projected[:, :model_width].reshape(item_count, row_count, -1, HEAD_DIM)
    key_rows = projected[:, model_width:2 * model_width].reshape(item_count, row_count, -1, HEAD_DIM)
    value_rows = projected[:, 2 * model_width:].reshape(item_count, row_count, -1, HEAD_DIM)
    heads_out = low(low_back(jax.checkpoint(attend)(queries, key_rows, value_rows, key_valid)))
    second = first + low_back(multiply(heads_out.reshape(row_total, model_width), w_proj))
    act_two = low(layer_norm(second, table[:, 2], table[:, 3]))
    pre_act = low_back(multiply(act_two, w_fc1))
    hidden = low(jax.nn.gelu(pre_act))
    return (second + multiply(hidden, w_fc2)).reshape(item_count, row_count, model_width)

def adam_step(grad, moment, square):
    new_mom = BETA_ONE * moment + (1.0 - BETA_ONE) * grad
    new_sq = BETA_TWO * square + (1.0 - BETA_TWO) * grad * grad
    step_dir = new_mom / (1.0 - BETA_ONE ** STEP) / (jnp.sqrt(new_sq / (1.0 - BETA_TWO ** STEP)) + EPS_ADAM)
    return (new_mom, new_sq, step_dir)

def reference(tokens, skip_store, cotangent, lengths, w_skip, mom_skip, sq_skip, w_qkv, mom_qkv, sq_qkv, w_proj, mom_proj, sq_proj, w_fc1, mom_fc1, sq_fc1, w_fc2, mom_fc2, sq_fc2, norm_table, norm_mom, norm_sq):
    params = (w_skip, w_qkv, w_proj, w_fc1, w_fc2, norm_table)
    groups = ITEMS // ITEMS_DEV
    token_groups = tokens.astype(jnp.float32).reshape(groups, ITEMS_DEV, SLOT, D)
    skip_groups = skip_store.astype(jnp.float32).reshape(groups, ITEMS_DEV, SLOT, D)
    cot_groups = cotangent.astype(jnp.float32).reshape(groups, ITEMS_DEV, SLOT, D)
    length_groups = lengths.reshape(groups, ITEMS_DEV)

    def one_group(carry, pieces):
        token_rows, skip_rows, cot_rows, group_lengths = pieces
        key_valid = jnp.arange(SLOT, dtype=jnp.int32)[None, :] < group_lengths[:, None]

        def run(param_set, token_part, skip_part):
            return block(param_set, token_part, skip_part, key_valid)
        out_rows, pull = jax.vjp(run, params, token_rows, skip_rows)
        param_grads, token_grads, skip_grads = pull(cot_rows)
        carry = jax.tree.map(jnp.add, carry, param_grads)
        return (carry, (out_rows.astype(jnp.bfloat16), token_grads.astype(jnp.bfloat16), skip_grads.astype(jnp.bfloat16)))
    zeros = tuple((jnp.zeros(param.shape, jnp.float32) for param in params))
    reduced, (out_all, token_all, skip_all) = lax.scan(one_group, zeros, (token_groups, skip_groups, cot_groups, length_groups))
    block_out = out_all.reshape(ITEMS, SLOT, D)
    grad_tokens = token_all.reshape(ITEMS, SLOT, D)
    grad_skip = skip_all.reshape(ITEMS, SLOT, D)
    masters = (w_skip, w_qkv, w_proj, w_fc1, w_fc2)
    momenta = (mom_skip, mom_qkv, mom_proj, mom_fc1, mom_fc2)
    seconds = (sq_skip, sq_qkv, sq_proj, sq_fc1, sq_fc2)
    renewed = []
    stat_cols = []
    for index in range(5):
        new_mom, new_sq, step_dir = adam_step(reduced[index], momenta[index], seconds[index])
        update = step_dir + DECAY * masters[index]
        weight_norm = jnp.sqrt(jnp.sum(masters[index] * masters[index]))
        update_norm = jnp.sqrt(jnp.sum(update * update))
        trust = weight_norm / (update_norm + EPS_ADAM)
        new_weight = masters[index] - RATE * trust * update
        renewed.append((new_weight, new_mom, new_sq, new_weight.astype(jnp.bfloat16)))
        stat_cols.append(jnp.stack([weight_norm, update_norm, trust]))
    table_mom, table_sq, table_step = adam_step(reduced[5], norm_mom, norm_sq)
    new_table = norm_table - RATE_TABLE * table_step
    lamb_stats = jnp.stack(stat_cols, 1)
    return (block_out, grad_tokens, grad_skip, renewed[0][0], renewed[0][1], renewed[0][2], renewed[0][3], renewed[1][0], renewed[1][1], renewed[1][2], renewed[1][3], renewed[2][0], renewed[2][1], renewed[2][2], renewed[2][3], renewed[3][0], renewed[3][1], renewed[3][2], renewed[3][3], renewed[4][0], renewed[4][1], renewed[4][2], renewed[4][3], new_table, table_mom, table_sq, lamb_stats)
```

```python
import functools
import math

import jax
import jax.numpy as jnp
from jax import lax
from jax.experimental import pallas as pl
from jax.experimental.pallas import tpu as pltpu
from jax.sharding import PartitionSpec as P

LOW = jnp.bfloat16
CHIP_X = 2
CHIP_Y = 2
CORES = 2


class Place:
    def __init__(self, wide, narrow):
        self.wide, self.narrow = wide, narrow
        self.depth = wide // CHIP_X
        at_wide, at_narrow = lax.axis_index("wide"), lax.axis_index("narrow")
        self.z, self.x = at_wide // CHIP_X, at_wide % CHIP_X
        self.y, self.c = at_narrow // CORES, at_narrow % CORES
        self.spot = jnp.stack([self.z, self.x, self.y, self.c]).astype(jnp.int32)

    def swap_x(self, value):
        return lax.ppermute(value, "wide", [(i, i ^ 1) for i in range(self.wide)])

    def swap_y(self, value):
        return lax.ppermute(value, "narrow", [(i, i ^ 2) for i in range(self.narrow)])

    def swap_c(self, value):
        return lax.ppermute(value, "narrow", [(i, i ^ 1) for i in range(self.narrow)])

    def up_z(self, value):
        return lax.ppermute(value, "wide", [(i, i + CHIP_X) for i in range(self.wide - CHIP_X)])

    def down_z(self, value):
        return lax.ppermute(value, "wide", [(i + CHIP_X, i) for i in range(self.wide - CHIP_X)])


def run_moves(name, place, inputs, out_shapes, plan):
    count = len(inputs)
    out_count = len(out_shapes)

    def body(spot_ref, *refs):
        ins, outs, sems = refs[:count], refs[count : count + out_count], refs[count + out_count]
        spot = [spot_ref[k] for k in range(4)]
        moves = plan(spot, ins, outs)
        for start in (True, False):
            for at, (when, source, target) in enumerate(moves):
                copy = pltpu.make_async_copy(source, target, sems.at[at])
                act = copy.start if start else copy.wait
                if when is None:
                    act()
                else:
                    pl.when(when)(act)

    return pl.pallas_call(
        body,
        out_shape=out_shapes,
        in_specs=[pl.BlockSpec(memory_space=pltpu.SMEM)] + [pl.BlockSpec(memory_space=pl.ANY)] * count,
        out_specs=[pl.BlockSpec(memory_space=pl.ANY)] * out_count,
        scratch_shapes=[pltpu.SemaphoreType.DMA((64,))],
        name=name,
    )(place.spot, *inputs)


def line_gather(place, piece):
    below, above = [piece], [piece]
    for _ in range(place.depth - 1):
        below.append(place.up_z(below[-1]))
        above.append(place.down_z(above[-1]))
    return piece, below[1:], above[1:]


def pack_line(place, piece, below, above, parts):
    depth = place.depth
    out = [jax.ShapeDtypeStruct((depth,) + piece.shape[1:], piece.dtype)] * parts

    def plan(spot, ins, outs):
        z = spot[0]
        moves = []
        for part in range(parts):
            moves.append((None, ins[0].at[part], outs[part].at[z]))
            for k in range(1, depth):
                moves.append((z >= k, ins[k].at[part], outs[part].at[jnp.maximum(z - k, 0)]))
                moves.append((z < depth - k, ins[depth - 1 + k].at[part], outs[part].at[jnp.minimum(z + k, depth - 1)]))
        return moves

    return run_moves("pack_line", place, [piece] + below + above, out, plan)


def plane_gather(place, first, second):
    first_pair = jnp.stack([first, place.swap_x(first)])
    second_pair = jnp.stack([second, place.swap_y(second)])
    return first_pair, place.swap_y(first_pair), second_pair, place.swap_x(second_pair)


def line_scatter(place, blocks):
    depth, z = place.depth, place.z

    def pick(at):
        return lax.dynamic_index_in_dim(blocks, jnp.clip(at, 0, depth - 1), 0, keepdims=False)

    up = down = None
    for k in range(depth - 1, 0, -1):
        up_part, down_part = pick(z + k), pick(z - k)
        if up is not None:
            up_part = (up_part.astype(jnp.float32) + up.astype(jnp.float32)).astype(LOW)
            down_part = (down_part.astype(jnp.float32) + down.astype(jnp.float32)).astype(LOW)
        up, down = place.up_z(up_part), place.down_z(down_part)
    return pick(z).astype(jnp.float32) + up.astype(jnp.float32) + down.astype(jnp.float32)


def added(mine, other):
    return (mine.astype(jnp.float32) + other.astype(jnp.float32)).astype(LOW)


def choose(value, axis, at):
    return lax.dynamic_index_in_dim(value, at, axis, keepdims=False)


def plane_scatter(place, first, second):
    x, y = place.x, place.y
    first_got = place.swap_x(choose(first, 1, 1 - x))
    second_got = place.swap_y(choose(second, 2, 1 - y))
    first_sum = added(choose(first, 1, x), first_got)
    second_sum = added(choose(second, 2, y), second_got)
    first_got = place.swap_y(choose(first_sum, 1, 1 - y))
    second_got = place.swap_x(choose(second_sum, 1, 1 - x))
    return added(choose(first_sum, 1, y), first_got), added(choose(second_sum, 1, x), second_got)


HEAD_DIM = 72
STEP = 10
EPS_NORM = 1e-05
BETA_ONE = 0.5
BETA_TWO = 0.5
EPS_ADAM = 1e-06
DECAY = 0.01
RATE = 0.5
RATE_TABLE = 0.1
NEGATIVE = -1e30
BOTH = ("wide", "narrow")
SKIP_CUT = 640


def project(left, right):
    return jnp.dot(left, right, preferred_element_type=jnp.float32)


def across(left, right):
    return lax.dot_general(
        left, right, (((0,), (0,)), ((), ())), preferred_element_type=jnp.float32
    )


def against(left, right):
    return lax.dot_general(
        left, right, (((1,), (1,)), ((), ())), preferred_element_type=jnp.float32
    )


def norm_stats(values):
    center = values - jnp.mean(values, -1, keepdims=True)
    inv_std = lax.rsqrt(jnp.mean(center * center, -1, keepdims=True) + EPS_NORM)
    return (center * inv_std, inv_std)


def norm_back(grad_out, normed, inv_std, gain_col):
    scaled = grad_out * gain_col
    return inv_std * (
        scaled
        - jnp.mean(scaled, -1, keepdims=True)
        - normed * jnp.mean(scaled * normed, -1, keepdims=True)
    )


def adam_step(grad, moment, square):
    new_mom = BETA_ONE * moment + (1.0 - BETA_ONE) * grad
    new_sq = BETA_TWO * square + (1.0 - BETA_TWO) * grad * grad
    step_dir = (
        new_mom / (1.0 - BETA_ONE**STEP) / (jnp.sqrt(new_sq / (1.0 - BETA_TWO**STEP)) + EPS_ADAM)
    )
    return (new_mom, new_sq, step_dir)


def halves_by_core(place, both):
    half = both.shape[1] // 2
    mine = lax.dynamic_slice_in_dim(both, place.c * half, half, 1)
    got = place.swap_c(lax.dynamic_slice_in_dim(both, (1 - place.c) * half, half, 1))
    first = place.c == 0
    return jnp.concatenate([jnp.where(first, mine, got), jnp.where(first, got, mine)], 0)


def gather_columns(place, block):
    unit = block.shape[1] // 2
    piece = jnp.stack([block[:, :unit], block[:, unit:]])
    first, second = pack_line(place, *line_gather(place, piece), 2)
    kept = plane_gather(place, first, second)
    return kept + tuple(place.swap_c(value) for value in kept)


def plane_moves(spot, kept, out_one, out_two, when_one=None, when_two=None):
    x, y = spot[1], spot[2]
    moves = []
    for turn in range(2):
        at = x if turn == 0 else 1 - x
        moves.append((when_one, kept[0].at[turn], out_one(at, y)))
        moves.append((when_one, kept[1].at[turn], out_one(at, 1 - y)))
        at = y if turn == 0 else 1 - y
        moves.append((when_two, kept[2].at[turn], out_two(x, at)))
        moves.append((when_two, kept[3].at[turn], out_two(1 - x, at)))
    return moves


def assemble_fc1(place, kept, rows, unit):
    depth = place.depth
    out = [jax.ShapeDtypeStruct((depth, CHIP_X, CHIP_Y, rows, 4 * unit), LOW)]

    def plan(spot, ins, outs):
        moves = []
        for core in range(2):
            at = spot[3] if core == 0 else 1 - spot[3]
            start = pl.multiple_of(at * (2 * unit), 128)

            def one(x, y, start=start):
                return outs[0].at[:, x, y, :, pl.ds(start, unit)]

            def two(x, y, start=start):
                return outs[0].at[:, x, y, :, pl.ds(start + unit, unit)]

            moves += plane_moves(spot, ins[4 * core : 4 * core + 4], one, two)
        return moves

    (full,) = run_moves("assemble_fc1", place, kept, out, plan)
    return full.reshape(depth * CHIP_X * CHIP_Y * rows, 4 * unit)


def assemble_qkvp(place, kept, rows, unit):
    depth = place.depth
    lead = (depth, CHIP_X, CHIP_Y, rows)
    out = [jax.ShapeDtypeStruct(lead + (3 * unit,), LOW), jax.ShapeDtypeStruct(lead + (unit,), LOW)]

    def plan(spot, ins, outs):
        moves = []
        for core in range(2):
            at = spot[3] if core == 0 else 1 - spot[3]
            start = pl.multiple_of(at * (2 * unit), 128)
            x, y = spot[1], spot[2]

            def one(x, y, start=start):
                return outs[0].at[:, x, y, :, pl.ds(start, unit)]

            def key(x, y):
                return outs[0].at[:, x, y, :, pl.ds(unit, unit)]

            def last(x, y):
                return outs[1].at[:, x, y]

            kept = ins[4 * core : 4 * core + 4]
            for turn, move in enumerate(plane_moves(spot, kept, one, key)):
                if turn % 4 < 2:
                    moves.append(move)
                else:
                    moves.append((at == 0, move[1], move[2]))
            for turn, move in enumerate(plane_moves(spot, kept, one, last)):
                if turn % 4 >= 2:
                    moves.append((at == 1, move[1], move[2]))
        return moves

    qkv, proj = run_moves("assemble_qkvp", place, kept, out, plan)
    total = depth * CHIP_X * CHIP_Y * rows
    return qkv.reshape(total, 3 * unit), proj.reshape(total, unit)


def gather_skip(place, low):
    piece = low[None]
    (line,) = pack_line(place, *line_gather(place, piece), 1)
    kept = plane_gather(place, line[:, :, :SKIP_CUT], line[:, :, SKIP_CUT:])
    kept = kept + tuple(place.swap_c(value) for value in kept)
    rows, cols = low.shape
    depth = place.depth
    out = [jax.ShapeDtypeStruct((depth, CHIP_X, CHIP_Y, CORES, rows, cols), LOW)]

    def plan(spot, ins, outs):
        moves = []
        for core in range(2):
            at = spot[3] if core == 0 else 1 - spot[3]

            def one(x, y, at=at):
                return outs[0].at[:, x, y, at, :, pl.ds(0, SKIP_CUT)]

            def two(x, y, at=at):
                return outs[0].at[:, x, y, at, :, pl.ds(SKIP_CUT, cols - SKIP_CUT)]

            moves += plane_moves(spot, ins[4 * core : 4 * core + 4], one, two)
        return moves

    (full,) = run_moves("assemble_skip", place, kept, out, plan)
    return full.reshape(depth * CHIP_X * CHIP_Y * CORES * rows, cols)


def gather_fc2(place, low):
    rows, cols = low.shape
    half = rows // 2
    kept = plane_gather(place, low[:half], low[half:])
    piece = jnp.concatenate(kept, 0)[None]
    (line,) = pack_line(place, *line_gather(place, piece), 1)
    other = place.swap_c(line)
    depth = place.depth
    out = [jax.ShapeDtypeStruct((depth, CHIP_X, CHIP_Y, CORES, 2, half, cols), LOW)]

    def plan(spot, ins, outs):
        x, y = spot[1], spot[2]
        moves = []
        for core in range(2):
            at = spot[3] if core == 0 else 1 - spot[3]
            for turn in range(2):
                to = x if turn == 0 else 1 - x
                moves.append((None, ins[core].at[:, turn], outs[0].at[:, to, y, at, 0]))
                moves.append((None, ins[core].at[:, 2 + turn], outs[0].at[:, to, 1 - y, at, 0]))
                to = y if turn == 0 else 1 - y
                moves.append((None, ins[core].at[:, 4 + turn], outs[0].at[:, x, to, at, 1]))
                moves.append((None, ins[core].at[:, 6 + turn], outs[0].at[:, 1 - x, to, at, 1]))
        return moves

    (full,) = run_moves("assemble_fc2", place, [line, other], out, plan)
    return full.reshape(depth * CHIP_X * CHIP_Y * CORES * rows, cols)


def gather_weights(place, lows):
    w_skip, w_qkv, w_proj, w_fc1, w_fc2 = lows
    if place.short:
        return tuple(lax.all_gather(low, BOTH, axis=0, tiled=True) for low in lows)
    rows, unit = 2 * w_proj.shape[0], w_proj.shape[1]
    skip = gather_skip(place, w_skip)
    pair = jnp.concatenate([w_qkv, w_proj], 1)
    qkv, proj = assemble_qkvp(place, gather_columns(place, halves_by_core(place, pair)), rows, unit)
    fc1 = assemble_fc1(place, gather_columns(place, halves_by_core(place, w_fc1)), rows, unit)
    fc2 = gather_fc2(place, w_fc2)
    return skip, qkv, proj, fc1, fc2


def blocks_of(place, grad):
    return grad.reshape(place.depth, CHIP_X, CHIP_Y, -1, grad.shape[-1])


def halves_to_rows(place, parts):
    rows = parts.shape[1] // 2
    keep = lax.dynamic_slice_in_dim(parts, place.c * rows, rows, 1)
    got = place.swap_c(lax.dynamic_slice_in_dim(parts, (1 - place.c) * rows, rows, 1))
    first = place.c == 0
    low, high = jnp.where(first, keep, got), jnp.where(first, got, keep)
    return jnp.concatenate([low[0], low[1], high[0], high[1]], 1)


def scatter_columns(place, sends, keeps):
    gots = [place.swap_c(across(*pair).astype(LOW)) for pair in sends]
    sums = [added(across(*pair), got) for pair, got in zip(keeps, gots)]
    lines = plane_scatter(place, *[blocks_of(place, value) for value in sums])
    return halves_to_rows(place, line_scatter(place, jnp.stack(lines, 1)))


def scatter_skip(place, joined, grad):
    sums = []
    for part in (grad[:, :SKIP_CUT], grad[:, SKIP_CUT:]):
        full = across(joined, part).astype(LOW)
        full = full.reshape(place.depth, CHIP_X, CHIP_Y, CORES, -1, part.shape[1])
        got = place.swap_c(choose(full, 3, 1 - place.c))
        sums.append(added(choose(full, 3, place.c), got))
    line = jnp.concatenate(plane_scatter(place, *sums), 2)
    return line_scatter(place, line)


def scatter_fc2(place, hidden, grad):
    full = across(hidden, grad).astype(LOW)
    rows = full.shape[0] // (place.depth * CHIP_X * CHIP_Y * CORES * 2)
    full = full.reshape(place.depth, CHIP_X, CHIP_Y, CORES, 2, rows, -1)
    got = place.swap_c(choose(full, 3, 1 - place.c))
    sums = added(choose(full, 3, place.c), got)
    plane = line_scatter(place, sums).astype(LOW)[None]
    first, second = plane_scatter(place, plane[:, :, :, 0], plane[:, :, :, 1])
    return jnp.concatenate([first[0], second[0]], 0).astype(jnp.float32)


def sum_small(value):
    return lax.psum(value, BOTH)


def local(
    short,
    wide,
    narrow,
    tokens,
    skip_store,
    cotangent,
    lengths,
    w_skip,
    mom_skip,
    sq_skip,
    w_qkv,
    mom_qkv,
    sq_qkv,
    w_proj,
    mom_proj,
    sq_proj,
    w_fc1,
    mom_fc1,
    sq_fc1,
    w_fc2,
    mom_fc2,
    sq_fc2,
    norm_table,
    norm_mom,
    norm_sq,
):
    place = Place(wide, narrow)
    place.short = short
    devices = wide * narrow
    masters = (w_skip, w_qkv, w_proj, w_fc1, w_fc2)
    momenta = (mom_skip, mom_qkv, mom_proj, mom_fc1, mom_fc2)
    seconds = (sq_skip, sq_qkv, sq_proj, sq_fc1, sq_fc2)
    model = tokens.shape[-1]

    token_rows = lax.all_to_all(tokens, "narrow", split_axis=0, concat_axis=1, tiled=True)
    skip_rows = lax.all_to_all(skip_store, "narrow", split_axis=0, concat_axis=2, tiled=True)
    cot_rows = lax.all_to_all(cotangent, "narrow", split_axis=0, concat_axis=1, tiled=True)
    items, slots = token_rows.shape[:2]
    rows = items * slots
    lengths = lax.dynamic_slice_in_dim(lengths, lax.axis_index("narrow") * items, items)

    table_low = norm_table.astype(LOW)
    spread = jnp.broadcast_to(table_low.reshape(1, -1), (devices, table_low.size))
    table = lax.all_to_all(spread, BOTH, 0, 0, tiled=True).reshape(model, 4).astype(jnp.float32)
    table = table.T

    lows = tuple(matrix.astype(LOW) for matrix in masters)
    full_skip, full_qkv, full_proj, full_fc1, full_fc2 = gather_weights(place, lows)

    joined = jnp.concatenate([token_rows, skip_rows], -1).reshape(rows, 2 * model)
    first = project(joined, full_skip)
    normed_one, inv_one = norm_stats(first)
    act_one = (normed_one * table[0] + table[1]).astype(LOW)
    projected = project(act_one, full_qkv).astype(LOW)
    heads = model // HEAD_DIM
    split = projected.reshape(items, slots, 3, heads, HEAD_DIM)
    queries, keys, values = split[:, :, 0], split[:, :, 1], split[:, :, 2]
    key_valid = jnp.arange(slots, dtype=jnp.int32)[None, :] < lengths[:, None]
    scale = 1.0 / math.sqrt(HEAD_DIM)
    logits = jnp.einsum("inhd,imhd->ihnm", queries, keys, preferred_element_type=jnp.float32) * scale
    logits = jnp.where(key_valid[:, None, None, :], logits, NEGATIVE)
    row_max = jnp.max(logits, -1, keepdims=True)
    log_total = row_max + jnp.log(jnp.sum(jnp.exp(logits - row_max), -1, keepdims=True))
    probs = jnp.exp(logits - log_total)
    probs_low = probs.astype(LOW)
    heads_out = (
        jnp.einsum("ihnm,imhd->inhd", probs_low, values, preferred_element_type=jnp.float32)
        .astype(LOW)
        .reshape(rows, model)
    )
    second = first + project(heads_out, full_proj)
    normed_two, inv_two = norm_stats(second)
    act_two = (normed_two * table[2] + table[3]).astype(LOW)
    pre_act = project(act_two, full_fc1)
    hidden = jax.nn.gelu(pre_act).astype(LOW)
    block_rows = (second + project(hidden, full_fc2)).astype(LOW).reshape(items, slots, model)
    block_out = lax.all_to_all(block_rows, "narrow", split_axis=1, concat_axis=0, tiled=True)

    grad_out = cot_rows.reshape(rows, model)
    if place.short:
        grad_fc2 = lax.psum_scatter(across(hidden, grad_out), BOTH, scatter_dimension=0, tiled=True)
    else:
        grad_fc2 = scatter_fc2(place, hidden, grad_out)
    _, gelu_pull = jax.vjp(jax.nn.gelu, pre_act)
    d_pre = gelu_pull(against(grad_out, full_fc2))[0].astype(LOW)
    if place.short:
        grad_fc1 = lax.psum_scatter(across(act_two, d_pre), BOTH, scatter_dimension=0, tiled=True)
    else:

        def cut(value, half, unit):
            return lax.dynamic_slice_in_dim(value, half * 2 * model + unit * model, model, 1)

        sends = [(act_two, cut(d_pre, 1 - place.c, unit)) for unit in range(2)]
        keeps = [(act_two, cut(d_pre, place.c, unit)) for unit in range(2)]
        grad_fc1 = scatter_columns(place, sends, keeps)
    d_act_two = against(d_pre, full_fc1)
    d_second = grad_out.astype(jnp.float32) + norm_back(d_act_two, normed_two, inv_two, table[2])
    d_second_low = d_second.astype(LOW)
    d_heads = against(d_second_low, full_proj).astype(LOW).reshape(items, slots, heads, HEAD_DIM)
    d_probs = jnp.einsum("inhd,imhd->ihnm", d_heads, values, preferred_element_type=jnp.float32)
    d_logits = (probs * (d_probs - jnp.sum(probs * d_probs, -1, keepdims=True))).astype(LOW)
    d_queries = jnp.einsum("ihnm,imhd->inhd", d_logits, keys, preferred_element_type=jnp.float32)
    d_keys = jnp.einsum("ihnm,inhd->imhd", d_logits, queries, preferred_element_type=jnp.float32)
    d_values = jnp.einsum("ihnm,inhd->imhd", probs_low, d_heads, preferred_element_type=jnp.float32)
    d_projected = jnp.concatenate(
        [
            (d_queries * scale).astype(LOW).reshape(rows, model),
            (d_keys * scale).astype(LOW).reshape(rows, model),
            d_values.astype(LOW).reshape(rows, model),
        ],
        -1,
    )
    if place.short:
        grad_qkv = lax.psum_scatter(across(act_one, d_projected), BOTH, scatter_dimension=0, tiled=True)
        grad_proj = lax.psum_scatter(across(heads_out, d_second_low), BOTH, scatter_dimension=0, tiled=True)
    else:

        def pair(half):
            left = jnp.where(half == 0, act_one, heads_out)
            key = d_projected[:, model : 2 * model]
            return [
                (act_one, lax.dynamic_slice_in_dim(d_projected, half * 2 * model, model, 1)),
                (left, jnp.where(half == 0, key, d_second_low)),
            ]

        both = scatter_columns(place, pair(1 - place.c), pair(place.c))
        grad_qkv, grad_proj = both[:, : 3 * model], both[:, 3 * model :]
    d_act_one = against(d_projected, full_qkv)
    d_first = d_second + norm_back(d_act_one, normed_one, inv_one, table[0])
    d_first_low = d_first.astype(LOW)
    if place.short:
        grad_skip_lin = lax.psum_scatter(across(joined, d_first_low), BOTH, scatter_dimension=0, tiled=True)
    else:
        grad_skip_lin = scatter_skip(place, joined, d_first_low)
    d_joined = against(d_first_low, full_skip).astype(LOW).reshape(items, slots, 2 * model)
    grad_tokens = lax.all_to_all(d_joined[:, :, :model], "narrow", split_axis=1, concat_axis=0, tiled=True)
    grad_skip = lax.all_to_all(d_joined[:, :, model:], "narrow", split_axis=2, concat_axis=0, tiled=True)

    table_grads = jnp.stack(
        [
            jnp.sum(d_act_one * normed_one, 0),
            jnp.sum(d_act_one, 0),
            jnp.sum(d_act_two * normed_two, 0),
            jnp.sum(d_act_two, 0),
        ],
        1,
    )
    table_parts = lax.all_to_all(table_grads.reshape(devices, -1), BOTH, 0, 0, tiled=True)
    table_grad = jnp.sum(table_parts, 0).reshape(norm_table.shape)

    reduced = (grad_skip_lin, grad_qkv, grad_proj, grad_fc1, grad_fc2)
    renewed = []
    update_list = []
    for index in range(5):
        new_mom, new_sq, step_dir = adam_step(reduced[index], momenta[index], seconds[index])
        update_list.append(step_dir + DECAY * masters[index])
        renewed.append((new_mom, new_sq))
    squares = [jnp.sum(matrix * matrix) for matrix in masters]
    squares += [jnp.sum(update * update) for update in update_list]
    squares = jnp.broadcast_to(jnp.stack(squares)[None, :], (devices, 10))
    totals = jnp.sum(lax.all_to_all(squares, BOTH, 0, 0, tiled=True), 0)
    weight_norm = jnp.sqrt(totals[:5])
    update_norm = jnp.sqrt(totals[5:])
    trust = weight_norm / (update_norm + EPS_ADAM)
    new_weights = [masters[index] - RATE * trust[index] * update_list[index] for index in range(5)]
    table_mom, table_sq, table_step = adam_step(table_grad, norm_mom, norm_sq)
    new_table = norm_table - RATE_TABLE * table_step
    lamb_stats = jnp.stack([weight_norm, update_norm, trust], 0)
    outs = [block_out, grad_tokens, grad_skip]
    for index in range(5):
        outs += [new_weights[index], *renewed[index], new_weights[index].astype(LOW)]
    return (*outs, new_table, table_mom, table_sq, lamb_stats)


def solution(mesh):
    wide, narrow = mesh.shape["wide"], mesh.shape["narrow"]
    short = not (wide == 8 and narrow == 4)
    rows = P("wide", "narrow", None)
    store = P("wide", None, "narrow")
    shard = P(BOTH, None)
    return jax.shard_map(
        functools.partial(local, short, wide, narrow),
        mesh=mesh,
        in_specs=(rows, store, rows, P("wide")) + (shard,) * 18,
        out_specs=(rows, rows, store) + (shard,) * 23 + (P(),),
        check_vma=False,
    )
```

```python
import functools
import math

import jax
import jax.numpy as jnp
from jax import lax
from jax.experimental import pallas as pl
from jax.experimental.pallas import tpu as pltpu
from jax.sharding import PartitionSpec as P

LOW = jnp.bfloat16
CHIP_X = 2
CHIP_Y = 2
CORES = 2


class Place:
    def __init__(self, wide, narrow):
        self.wide, self.narrow = wide, narrow
        self.depth = wide // CHIP_X
        at_wide, at_narrow = lax.axis_index("wide"), lax.axis_index("narrow")
        self.z, self.x = at_wide // CHIP_X, at_wide % CHIP_X
        self.y, self.c = at_narrow // CORES, at_narrow % CORES
        self.spot = jnp.stack([self.z, self.x, self.y, self.c]).astype(jnp.int32)
        self.last = {}

    def turn(self, kind, values, hops):
        before = self.last.get(kind, ())
        values = lax.optimization_barrier((*values, *before))[: len(values)]
        self.last[kind] = tuple(hop(value) for hop, value in zip(hops, values))
        return self.last[kind]

    def swap_x(self, value):
        return lax.ppermute(value, "wide", [(i, i ^ 1) for i in range(self.wide)])

    def swap_y(self, value):
        return lax.ppermute(value, "narrow", [(i, i ^ 2) for i in range(self.narrow)])

    def swap_c(self, value):
        return lax.ppermute(value, "narrow", [(i, i ^ 1) for i in range(self.narrow)])

    def up_z(self, value):
        return lax.ppermute(value, "wide", [(i, i + CHIP_X) for i in range(self.wide - CHIP_X)])

    def down_z(self, value):
        return lax.ppermute(value, "wide", [(i + CHIP_X, i) for i in range(self.wide - CHIP_X)])


def run_moves(name, place, inputs, out_shapes, plan):
    count = len(inputs)
    out_count = len(out_shapes)

    def body(spot_ref, *refs):
        ins, outs, sems = refs[:count], refs[count : count + out_count], refs[count + out_count]
        spot = [spot_ref[k] for k in range(4)]
        moves = plan(spot, ins, outs)
        for start in (True, False):
            for at, (when, source, target) in enumerate(moves):
                copy = pltpu.make_async_copy(source, target, sems.at[at])
                act = copy.start if start else copy.wait
                if when is None:
                    act()
                else:
                    pl.when(when)(act)

    return pl.pallas_call(
        body,
        out_shape=out_shapes,
        in_specs=[pl.BlockSpec(memory_space=pltpu.SMEM)] + [pl.BlockSpec(memory_space=pl.ANY)] * count,
        out_specs=[pl.BlockSpec(memory_space=pltpu.VMEM)] * out_count,
        scratch_shapes=[pltpu.SemaphoreType.DMA((64,))],
        compiler_params=pltpu.CompilerParams(vmem_limit_bytes=40 * 1024 * 1024),
        name=name,
    )(place.spot, *inputs)


def line_gather(place, piece):
    below, above = [piece], [piece]
    for _ in range(place.depth - 1):
        low, high = place.turn("z", (below[-1], above[-1]), (place.up_z, place.down_z))
        below.append(low)
        above.append(high)
    return piece, below[1:], above[1:]


def pack_line(place, piece, below, above, parts):
    depth = place.depth
    out = [jax.ShapeDtypeStruct((depth,) + piece.shape[1:], piece.dtype)] * parts

    def plan(spot, ins, outs):
        z = spot[0]
        moves = []
        for part in range(parts):
            moves.append((None, ins[0].at[part], outs[part].at[z]))
            for k in range(1, depth):
                moves.append((z >= k, ins[k].at[part], outs[part].at[jnp.maximum(z - k, 0)]))
                moves.append((z < depth - k, ins[depth - 1 + k].at[part], outs[part].at[jnp.minimum(z + k, depth - 1)]))
        return moves

    return run_moves("pack_line", place, [piece] + below + above, out, plan)


def plane_gather(place, first, second):
    first_got, second_got = place.turn("plane", (first, second), (place.swap_x, place.swap_y))
    first_pair = jnp.stack([first, first_got])
    second_pair = jnp.stack([second, second_got])
    first_far, second_far = place.turn("plane", (first_pair, second_pair), (place.swap_y, place.swap_x))
    return first_pair, first_far, second_pair, second_far


def line_scatter(place, blocks):
    depth, z = place.depth, place.z

    def pick(at):
        return lax.dynamic_index_in_dim(blocks, jnp.clip(at, 0, depth - 1), 0, keepdims=False)

    up = down = None
    for k in range(depth - 1, 0, -1):
        up_part, down_part = pick(z + k), pick(z - k)
        if up is not None:
            up_part = (up_part.astype(jnp.float32) + up.astype(jnp.float32)).astype(LOW)
            down_part = (down_part.astype(jnp.float32) + down.astype(jnp.float32)).astype(LOW)
        up, down = place.turn("z", (up_part, down_part), (place.up_z, place.down_z))
    return pick(z).astype(jnp.float32) + up.astype(jnp.float32) + down.astype(jnp.float32)


def added(mine, other):
    return (mine.astype(jnp.float32) + other.astype(jnp.float32)).astype(LOW)


def choose(value, axis, at):
    return lax.dynamic_index_in_dim(value, at, axis, keepdims=False)


def plane_scatter(place, first, second):
    x, y = place.x, place.y
    parts = (choose(first, 1, 1 - x), choose(second, 2, 1 - y))
    first_got, second_got = place.turn("plane", parts, (place.swap_x, place.swap_y))
    first_sum = added(choose(first, 1, x), first_got)
    second_sum = added(choose(second, 2, y), second_got)
    parts = (choose(first_sum, 1, 1 - y), choose(second_sum, 1, 1 - x))
    first_got, second_got = place.turn("plane", parts, (place.swap_y, place.swap_x))
    return added(choose(first_sum, 1, y), first_got), added(choose(second_sum, 1, x), second_got)


HEAD_DIM = 72
STEP = 10
EPS_NORM = 1e-05
BETA_ONE = 0.5
BETA_TWO = 0.5
EPS_ADAM = 1e-06
DECAY = 0.01
RATE = 0.5
RATE_TABLE = 0.1
NEGATIVE = -1e30
BOTH = ("wide", "narrow")
SKIP_CUT = 640


def project(left, right):
    return jnp.dot(left, right, preferred_element_type=jnp.float32)


def across(left, right):
    return lax.dot_general(
        left, right, (((0,), (0,)), ((), ())), preferred_element_type=jnp.float32
    )


def against(left, right):
    return lax.dot_general(
        left, right, (((1,), (1,)), ((), ())), preferred_element_type=jnp.float32
    )


def norm_stats(values):
    center = values - jnp.mean(values, -1, keepdims=True)
    inv_std = lax.rsqrt(jnp.mean(center * center, -1, keepdims=True) + EPS_NORM)
    return (center * inv_std, inv_std)


def norm_back(grad_out, normed, inv_std, gain_col):
    scaled = grad_out * gain_col
    return inv_std * (
        scaled
        - jnp.mean(scaled, -1, keepdims=True)
        - normed * jnp.mean(scaled * normed, -1, keepdims=True)
    )


def adam_step(grad, moment, square):
    new_mom = BETA_ONE * moment + (1.0 - BETA_ONE) * grad
    new_sq = BETA_TWO * square + (1.0 - BETA_TWO) * grad * grad
    step_dir = (
        new_mom / (1.0 - BETA_ONE**STEP) / (jnp.sqrt(new_sq / (1.0 - BETA_TWO**STEP)) + EPS_ADAM)
    )
    return (new_mom, new_sq, step_dir)


ATTN_VMEM = 48 * 1024 * 1024


def head_window(head):
    start = head * HEAD_DIM
    base = start // 128 * 128
    width = 128 if start - base + HEAD_DIM <= 128 else 256
    return base, width, start - base


def lane_mask(rows, width, offset):
    lane = lax.broadcasted_iota(jnp.int32, (rows, width), 1)
    return (lane >= offset) & (lane < offset + HEAD_DIM)


def score_rows(queries, keys, length, slots):
    logits = against(keys, queries) * (1.0 / math.sqrt(HEAD_DIM))
    key_at = lax.broadcasted_iota(jnp.int32, (slots, slots), 0)
    return jnp.where(key_at < length, logits, NEGATIVE)


def rows_of(ref, window):
    return ref[:, 0, :, window].reshape(-1, window.size)


def put_rows(ref, window, mask, value):
    merged = jnp.where(mask, value, rows_of(ref, window))
    ref[:, 0, :, window] = merged.reshape(ref.shape[0], ref.shape[2], window.size)


def attend_kernel(model, lengths_ref, qkv_ref, out_ref, lse_ref):
    slots = qkv_ref.shape[0] * qkv_ref.shape[2]
    length = lengths_ref[pl.program_id(0)]
    for head in range(model // HEAD_DIM):
        base, width, offset = head_window(head)
        mask = lane_mask(slots, width, offset)
        window = pl.ds(base, width)
        queries = jnp.where(mask, rows_of(qkv_ref, window), jnp.zeros((), LOW))
        logits = score_rows(queries, rows_of(qkv_ref, pl.ds(model + base, width)), length, slots)
        top = jnp.max(logits, 0, keepdims=True)
        lse = top + jnp.log(jnp.sum(jnp.exp(logits - top), 0, keepdims=True))
        probs = jnp.exp(logits - lse).astype(LOW)
        lse_ref[0, pl.ds(head, 1), :] = lse
        heads_out = across(probs, rows_of(qkv_ref, pl.ds(2 * model + base, width))).astype(LOW)
        put_rows(out_ref, window, mask, heads_out)


def attend_back_kernel(model, lengths_ref, qkv_ref, d_heads_ref, lse_ref, out_ref):
    slots = qkv_ref.shape[0] * qkv_ref.shape[2]
    length = lengths_ref[pl.program_id(0)]
    scale = 1.0 / math.sqrt(HEAD_DIM)
    for head in range(model // HEAD_DIM):
        base, width, offset = head_window(head)
        mask = lane_mask(slots, width, offset)
        window = pl.ds(base, width)
        key_window = pl.ds(model + base, width)
        value_window = pl.ds(2 * model + base, width)
        zero = jnp.zeros((), LOW)
        queries = jnp.where(mask, rows_of(qkv_ref, window), zero)
        d_heads = jnp.where(mask, rows_of(d_heads_ref, window), zero)
        keys = rows_of(qkv_ref, key_window)
        logits = score_rows(queries, keys, length, slots)
        probs = jnp.exp(logits - lse_ref[0, pl.ds(head, 1), :])
        d_probs = against(rows_of(qkv_ref, value_window), d_heads)
        weighted = probs * d_probs
        d_logits = (weighted - probs * jnp.sum(weighted, 0, keepdims=True)).astype(LOW)
        d_queries = (across(d_logits, keys) * scale).astype(LOW)
        d_keys = (project(d_logits, queries) * scale).astype(LOW)
        d_values = project(probs.astype(LOW), d_heads).astype(LOW)
        put_rows(out_ref, window, mask, d_queries)
        put_rows(out_ref, key_window, mask, d_keys)
        put_rows(out_ref, value_window, mask, d_values)


def item_block(parts, part, cols):
    return pl.BlockSpec((parts, 1, part, cols), lambda i: (0, i, 0, 0))


def lse_block(heads, slots):
    return pl.BlockSpec((1, heads, slots), lambda i: (i, 0, 0))


def attend(lengths, qkv, model):
    parts, items, part = qkv.shape[:3]
    slots = parts * part
    heads = model // HEAD_DIM
    return pl.pallas_call(
        functools.partial(attend_kernel, model),
        grid=(items,),
        out_shape=[
            jax.ShapeDtypeStruct((parts, items, part, model), LOW),
            jax.ShapeDtypeStruct((items, heads, slots), jnp.float32),
        ],
        in_specs=[pl.BlockSpec(memory_space=pltpu.SMEM), item_block(parts, part, 3 * model)],
        out_specs=[item_block(parts, part, model), lse_block(heads, slots)],
        compiler_params=pltpu.CompilerParams(vmem_limit_bytes=ATTN_VMEM),
        name="attend",
    )(lengths, qkv)


def attend_back(lengths, qkv, d_heads, lse, model):
    parts, items, part = qkv.shape[:3]
    slots = parts * part
    heads = model // HEAD_DIM
    return pl.pallas_call(
        functools.partial(attend_back_kernel, model),
        grid=(items,),
        out_shape=jax.ShapeDtypeStruct((parts, items, part, 3 * model), LOW),
        in_specs=[
            pl.BlockSpec(memory_space=pltpu.SMEM),
            item_block(parts, part, 3 * model),
            item_block(parts, part, model),
            lse_block(heads, slots),
        ],
        out_specs=item_block(parts, part, 3 * model),
        compiler_params=pltpu.CompilerParams(vmem_limit_bytes=ATTN_VMEM),
        name="attend_back",
    )(lengths, qkv, d_heads, lse)


def halves_by_core(place, both):
    half = both.shape[2] // 2
    mine = lax.dynamic_slice_in_dim(both, place.c * half, half, 2)
    got = place.swap_c(lax.dynamic_slice_in_dim(both, (1 - place.c) * half, half, 2))
    first = place.c == 0
    return jnp.concatenate([jnp.where(first, mine, got), jnp.where(first, got, mine)], 1)


def gather_columns(place, block):
    unit = block.shape[1] // 2
    piece = jnp.stack([block[:, :unit], block[:, unit:]])
    first, second = pack_line(place, *line_gather(place, piece), 2)
    kept = plane_gather(place, first, second)
    return kept + tuple(place.swap_c(value) for value in kept)


def plane_moves(spot, kept, out_one, out_two, when_one=None, when_two=None):
    x, y = spot[1], spot[2]
    moves = []
    for turn in range(2):
        at = x if turn == 0 else 1 - x
        moves.append((when_one, kept[0].at[turn], out_one(at, y)))
        moves.append((when_one, kept[1].at[turn], out_one(at, 1 - y)))
        at = y if turn == 0 else 1 - y
        moves.append((when_two, kept[2].at[turn], out_two(x, at)))
        moves.append((when_two, kept[3].at[turn], out_two(1 - x, at)))
    return moves


def assemble_fc1(place, kept, rows, unit):
    depth = place.depth
    out = [jax.ShapeDtypeStruct((depth, CHIP_X, CHIP_Y, rows, 4 * unit), LOW)]

    def plan(spot, ins, outs):
        moves = []
        for core in range(2):
            at = spot[3] if core == 0 else 1 - spot[3]
            start = pl.multiple_of(at * (2 * unit), 128)

            def one(x, y, start=start):
                return outs[0].at[:, x, y, :, pl.ds(start, unit)]

            def two(x, y, start=start):
                return outs[0].at[:, x, y, :, pl.ds(start + unit, unit)]

            moves += plane_moves(spot, ins[4 * core : 4 * core + 4], one, two)
        return moves

    (full,) = run_moves("assemble_fc1", place, kept, out, plan)
    return full.reshape(depth * CHIP_X * CHIP_Y * rows, 4 * unit)


def assemble_qkvp(place, kept, rows, unit):
    depth = place.depth
    lead = (depth, CHIP_X, CHIP_Y, rows)
    out = [jax.ShapeDtypeStruct(lead + (3 * unit,), LOW), jax.ShapeDtypeStruct(lead + (unit,), LOW)]

    def plan(spot, ins, outs):
        moves = []
        for core in range(2):
            at = spot[3] if core == 0 else 1 - spot[3]
            start = pl.multiple_of(at * (2 * unit), 128)
            x, y = spot[1], spot[2]

            def one(x, y, start=start):
                return outs[0].at[:, x, y, :, pl.ds(start, unit)]

            def key(x, y):
                return outs[0].at[:, x, y, :, pl.ds(unit, unit)]

            def last(x, y):
                return outs[1].at[:, x, y]

            kept = ins[4 * core : 4 * core + 4]
            for turn, move in enumerate(plane_moves(spot, kept, one, key)):
                if turn % 4 < 2:
                    moves.append(move)
                else:
                    moves.append((at == 0, move[1], move[2]))
            for turn, move in enumerate(plane_moves(spot, kept, one, last)):
                if turn % 4 >= 2:
                    moves.append((at == 1, move[1], move[2]))
        return moves

    qkv, proj = run_moves("assemble_qkvp", place, kept, out, plan)
    total = depth * CHIP_X * CHIP_Y * rows
    return qkv.reshape(total, 3 * unit), proj.reshape(total, unit)


def gather_skip(place, low):
    piece = low[None]
    (line,) = pack_line(place, *line_gather(place, piece), 1)
    kept = plane_gather(place, line[:, :, :SKIP_CUT], line[:, :, SKIP_CUT:])
    kept = kept + tuple(place.swap_c(value) for value in kept)
    rows, cols = low.shape
    depth = place.depth
    out = [jax.ShapeDtypeStruct((depth, CHIP_X, CHIP_Y, CORES, rows, cols), LOW)]

    def plan(spot, ins, outs):
        moves = []
        for core in range(2):
            at = spot[3] if core == 0 else 1 - spot[3]

            def one(x, y, at=at):
                return outs[0].at[:, x, y, at, :, pl.ds(0, SKIP_CUT)]

            def two(x, y, at=at):
                return outs[0].at[:, x, y, at, :, pl.ds(SKIP_CUT, cols - SKIP_CUT)]

            moves += plane_moves(spot, ins[4 * core : 4 * core + 4], one, two)
        return moves

    (full,) = run_moves("assemble_skip", place, kept, out, plan)
    return full.reshape(depth * CHIP_X * CHIP_Y * CORES * rows, cols)


def gather_fc2(place, low, kept):
    rows, cols = low.shape
    half = rows // 2
    piece = jnp.concatenate(kept, 0)[None]
    (line,) = pack_line(place, *line_gather(place, piece), 1)
    other = place.swap_c(line)
    depth = place.depth
    out = [jax.ShapeDtypeStruct((depth, CHIP_X, CHIP_Y, CORES, 2, half, cols), LOW)]

    def plan(spot, ins, outs):
        x, y = spot[1], spot[2]
        moves = []
        for core in range(2):
            at = spot[3] if core == 0 else 1 - spot[3]
            for turn in range(2):
                to = x if turn == 0 else 1 - x
                moves.append((None, ins[core].at[:, turn], outs[0].at[:, to, y, at, 0]))
                moves.append((None, ins[core].at[:, 2 + turn], outs[0].at[:, to, 1 - y, at, 0]))
                to = y if turn == 0 else 1 - y
                moves.append((None, ins[core].at[:, 4 + turn], outs[0].at[:, x, to, at, 1]))
                moves.append((None, ins[core].at[:, 6 + turn], outs[0].at[:, 1 - x, to, at, 1]))
        return moves

    (full,) = run_moves("assemble_fc2", place, [line, other], out, plan)
    return full.reshape(depth * CHIP_X * CHIP_Y * CORES * rows, cols)


def gather_weights(place, lows):
    w_skip, w_qkv, w_proj, w_fc1, w_fc2 = lows
    if place.short:
        return tuple(lax.all_gather(low, BOTH, axis=0, tiled=True) for low in lows)
    rows, unit = 2 * w_proj.shape[0], w_proj.shape[1]
    pair = halves_by_core(place, jnp.stack([jnp.concatenate([w_qkv, w_proj], 1), w_fc1]))
    half = w_fc2.shape[0] // 2
    plane = plane_gather(place, w_fc2[:half], w_fc2[half:])
    skip = gather_skip(place, w_skip)
    qkv, proj = assemble_qkvp(place, gather_columns(place, pair[0]), rows, unit)
    fc1 = assemble_fc1(place, gather_columns(place, pair[1]), rows, unit)
    fc2 = gather_fc2(place, w_fc2, plane)
    return skip, qkv, proj, fc1, fc2


def blocks_of(place, grad):
    return grad.reshape(place.depth, CHIP_X, CHIP_Y, -1, grad.shape[-1])


def halves_to_rows(place, parts):
    rows = parts.shape[1] // 2
    keep = lax.dynamic_slice_in_dim(parts, place.c * rows, rows, 1)
    got = place.swap_c(lax.dynamic_slice_in_dim(parts, (1 - place.c) * rows, rows, 1))
    first = place.c == 0
    low, high = jnp.where(first, keep, got), jnp.where(first, got, keep)
    return jnp.concatenate([low[0], low[1], high[0], high[1]], 1)


def scatter_columns(place, sends, keeps):
    gots = [place.swap_c(across(*pair).astype(LOW)) for pair in sends]
    sums = [added(across(*pair), got) for pair, got in zip(keeps, gots)]
    lines = plane_scatter(place, *[blocks_of(place, value) for value in sums])
    return halves_to_rows(place, line_scatter(place, jnp.stack(lines, 1)))


def scatter_skip(place, joined, grad):
    sums = []
    for part in (grad[:, :SKIP_CUT], grad[:, SKIP_CUT:]):
        full = across(joined, part).astype(LOW)
        full = full.reshape(place.depth, CHIP_X, CHIP_Y, CORES, -1, part.shape[1])
        got = place.swap_c(choose(full, 3, 1 - place.c))
        sums.append(added(choose(full, 3, place.c), got))
    line = jnp.concatenate(plane_scatter(place, *sums), 2)
    return line_scatter(place, line)


def scatter_fc2(place, hidden, grad):
    full = across(hidden, grad).astype(LOW)
    rows = full.shape[0] // (place.depth * CHIP_X * CHIP_Y * CORES * 2)
    full = full.reshape(place.depth, CHIP_X, CHIP_Y, CORES, 2, rows, -1)
    got = place.swap_c(choose(full, 3, 1 - place.c))
    sums = added(choose(full, 3, place.c), got)
    plane = line_scatter(place, sums).astype(LOW)[None]
    first, second = plane_scatter(place, plane[:, :, :, 0], plane[:, :, :, 1])
    return jnp.concatenate([first[0], second[0]], 0).astype(jnp.float32)


def sum_small(value):
    return lax.psum(value, BOTH)


def local(
    short,
    wide,
    narrow,
    tokens,
    skip_store,
    cotangent,
    lengths,
    w_skip,
    mom_skip,
    sq_skip,
    w_qkv,
    mom_qkv,
    sq_qkv,
    w_proj,
    mom_proj,
    sq_proj,
    w_fc1,
    mom_fc1,
    sq_fc1,
    w_fc2,
    mom_fc2,
    sq_fc2,
    norm_table,
    norm_mom,
    norm_sq,
):
    place = Place(wide, narrow)
    place.short = short
    devices = wide * narrow
    masters = (w_skip, w_qkv, w_proj, w_fc1, w_fc2)
    momenta = (mom_skip, mom_qkv, mom_proj, mom_fc1, mom_fc2)
    seconds = (sq_skip, sq_qkv, sq_proj, sq_fc1, sq_fc2)
    model = tokens.shape[-1]

    items, part = tokens.shape[0] // narrow, tokens.shape[1]
    slots = narrow * part
    rows = items * slots

    def swap_items(value):
        value = value.reshape(narrow, items, *value.shape[1:])
        return lax.all_to_all(value, "narrow", 0, 0, tiled=True)

    token_rows = swap_items(tokens).reshape(rows, model)
    skip_rows = swap_items(skip_store).reshape(narrow, items, narrow, part, model // narrow)
    skip_rows = skip_rows.transpose(2, 1, 3, 0, 4).reshape(rows, model)
    cot_rows = swap_items(cotangent)
    lengths = lax.dynamic_slice_in_dim(lengths, lax.axis_index("narrow") * items, items)

    table_low = norm_table.astype(LOW)
    spread = jnp.broadcast_to(table_low.reshape(1, -1), (devices, table_low.size))
    table = lax.all_to_all(spread, BOTH, 0, 0, tiled=True).reshape(model, 4).astype(jnp.float32)
    table = table.T

    lows = tuple(matrix.astype(LOW) for matrix in masters)
    full_skip, full_qkv, full_proj, full_fc1, full_fc2 = gather_weights(place, lows)

    joined = jnp.concatenate([token_rows, skip_rows], -1)
    first = project(joined, full_skip)
    normed_one, inv_one = norm_stats(first)
    act_one = (normed_one * table[0] + table[1]).astype(LOW)
    projected = project(act_one, full_qkv).astype(LOW)
    qkv = projected.reshape(narrow, items, part, 3 * model)
    heads_out, lse = attend(lengths, qkv, model)
    heads_out = heads_out.reshape(rows, model)
    second = first + project(heads_out, full_proj)
    normed_two, inv_two = norm_stats(second)
    act_two = (normed_two * table[2] + table[3]).astype(LOW)
    pre_act = project(act_two, full_fc1)
    hidden = jax.nn.gelu(pre_act).astype(LOW)
    block_rows = (second + project(hidden, full_fc2)).astype(LOW)

    def swap_back(value):
        value = value.reshape(narrow, items, part, model)
        return lax.all_to_all(value, "narrow", 0, 0, tiled=True).reshape(narrow * items, part, model)

    block_out = swap_back(block_rows)

    grad_out = cot_rows.reshape(rows, model)
    if place.short:
        grad_fc2 = lax.psum_scatter(across(hidden, grad_out), BOTH, scatter_dimension=0, tiled=True)
    else:
        grad_fc2 = scatter_fc2(place, hidden, grad_out)
    _, gelu_pull = jax.vjp(jax.nn.gelu, pre_act)
    d_pre = gelu_pull(against(grad_out, full_fc2))[0].astype(LOW)
    if place.short:
        grad_fc1 = lax.psum_scatter(across(act_two, d_pre), BOTH, scatter_dimension=0, tiled=True)
    else:

        def cut(value, half, unit):
            return lax.dynamic_slice_in_dim(value, half * 2 * model + unit * model, model, 1)

        sends = [(act_two, cut(d_pre, 1 - place.c, unit)) for unit in range(2)]
        keeps = [(act_two, cut(d_pre, place.c, unit)) for unit in range(2)]
        grad_fc1 = scatter_columns(place, sends, keeps)
    d_act_two = against(d_pre, full_fc1)
    d_second = grad_out.astype(jnp.float32) + norm_back(d_act_two, normed_two, inv_two, table[2])
    d_second_low = d_second.astype(LOW)
    d_heads = against(d_second_low, full_proj).astype(LOW).reshape(narrow, items, part, model)
    d_projected = attend_back(lengths, qkv, d_heads, lse, model).reshape(rows, 3 * model)
    if place.short:
        grad_qkv = lax.psum_scatter(across(act_one, d_projected), BOTH, scatter_dimension=0, tiled=True)
        grad_proj = lax.psum_scatter(across(heads_out, d_second_low), BOTH, scatter_dimension=0, tiled=True)
    else:

        def pair(half):
            left = jnp.where(half == 0, act_one, heads_out)
            key = d_projected[:, model : 2 * model]
            return [
                (act_one, lax.dynamic_slice_in_dim(d_projected, half * 2 * model, model, 1)),
                (left, jnp.where(half == 0, key, d_second_low)),
            ]

        both = scatter_columns(place, pair(1 - place.c), pair(place.c))
        grad_qkv, grad_proj = both[:, : 3 * model], both[:, 3 * model :]
    d_act_one = against(d_projected, full_qkv)
    d_first = d_second + norm_back(d_act_one, normed_one, inv_one, table[0])
    d_first_low = d_first.astype(LOW)
    if place.short:
        grad_skip_lin = lax.psum_scatter(across(joined, d_first_low), BOTH, scatter_dimension=0, tiled=True)
    else:
        grad_skip_lin = scatter_skip(place, joined, d_first_low)
    d_joined = against(d_first_low, full_skip).astype(LOW)
    grad_tokens = swap_back(d_joined[:, :model])
    d_skip = d_joined[:, model:].reshape(narrow, items, part, narrow, model // narrow)
    d_skip = d_skip.transpose(3, 1, 0, 2, 4).reshape(narrow, items, slots, model // narrow)
    grad_skip = lax.all_to_all(d_skip, "narrow", 0, 0, tiled=True).reshape(skip_store.shape)

    table_grads = jnp.stack(
        [
            jnp.sum(d_act_one * normed_one, 0),
            jnp.sum(d_act_one, 0),
            jnp.sum(d_act_two * normed_two, 0),
            jnp.sum(d_act_two, 0),
        ],
        1,
    )
    table_parts = lax.all_to_all(table_grads.reshape(devices, -1), BOTH, 0, 0, tiled=True)
    table_grad = jnp.sum(table_parts, 0).reshape(norm_table.shape)

    reduced = (grad_skip_lin, grad_qkv, grad_proj, grad_fc1, grad_fc2)
    renewed = []
    update_list = []
    for index in range(5):
        new_mom, new_sq, step_dir = adam_step(reduced[index], momenta[index], seconds[index])
        update_list.append(step_dir + DECAY * masters[index])
        renewed.append((new_mom, new_sq))
    squares = [jnp.sum(matrix * matrix) for matrix in masters]
    squares += [jnp.sum(update * update) for update in update_list]
    squares = jnp.broadcast_to(jnp.stack(squares)[None, :], (devices, 10))
    totals = jnp.sum(lax.all_to_all(squares, BOTH, 0, 0, tiled=True), 0)
    weight_norm = jnp.sqrt(totals[:5])
    update_norm = jnp.sqrt(totals[5:])
    trust = weight_norm / (update_norm + EPS_ADAM)
    new_weights = [masters[index] - RATE * trust[index] * update_list[index] for index in range(5)]
    table_mom, table_sq, table_step = adam_step(table_grad, norm_mom, norm_sq)
    new_table = norm_table - RATE_TABLE * table_step
    lamb_stats = jnp.stack([weight_norm, update_norm, trust], 0)
    outs = [block_out, grad_tokens, grad_skip]
    for index in range(5):
        outs += [new_weights[index], *renewed[index], new_weights[index].astype(LOW)]
    return (*outs, new_table, table_mom, table_sq, lamb_stats)


def solution(mesh):
    wide, narrow = mesh.shape["wide"], mesh.shape["narrow"]
    short = not (wide == 8 and narrow == 4)
    rows = P("wide", "narrow", None)
    store = P("wide", None, "narrow")
    shard = P(BOTH, None)
    return jax.shard_map(
        functools.partial(local, short, wide, narrow),
        mesh=mesh,
        in_specs=(rows, store, rows, P("wide")) + (shard,) * 18,
        out_specs=(rows, rows, store) + (shard,) * 23 + (P(),),
        check_vma=False,
    )
```

```python
import functools
import math

import jax
import jax.numpy as jnp
from jax import lax
from jax.experimental import pallas as pl
from jax.experimental.pallas import tpu as pltpu
from jax.sharding import PartitionSpec as P

LOW = jnp.bfloat16
CHIP_X = 2
CHIP_Y = 2
CORES = 2
SEMAPHORES = 128


class Place:
    def __init__(self, wide, narrow):
        self.wide, self.narrow = wide, narrow
        self.depth = wide // CHIP_X
        at_wide, at_narrow = lax.axis_index("wide"), lax.axis_index("narrow")
        self.z, self.x = at_wide // CHIP_X, at_wide % CHIP_X
        self.y, self.c = at_narrow // CORES, at_narrow % CORES
        self.n = at_narrow
        self.spot = jnp.stack([self.z, self.x, self.y, self.c, self.n]).astype(jnp.int32)

    def swap_x(self, value):
        return lax.ppermute(value, "wide", [(i, i ^ 1) for i in range(self.wide)])

    def swap_y(self, value):
        return lax.ppermute(value, "narrow", [(i, i ^ 2) for i in range(self.narrow)])

    def swap_c(self, value):
        return lax.ppermute(value, "narrow", [(i, i ^ 1) for i in range(self.narrow)])

    def swap_z(self, turn):
        pairs = [(i, i ^ (turn * CHIP_X)) for i in range(self.wide)]
        return lambda value: lax.ppermute(value, "wide", pairs)


def run_moves(name, place, inputs, out_shapes, plan, stage=False):
    count = len(inputs)
    out_count = len(out_shapes)

    def body(spot_ref, *refs):
        ins, outs, sems = refs[:count], refs[count : count + out_count], refs[count + out_count]
        held = refs[count + out_count + 1 :] if stage else outs
        spot = [spot_ref[k] for k in range(5)]
        moves = plan(spot, ins, held)
        assert len(moves) + out_count <= SEMAPHORES
        for start in (True, False):
            for at, (when, source, target) in enumerate(moves):
                copy = pltpu.make_async_copy(source, target, sems.at[at])
                act = copy.start if start else copy.wait
                if when is None:
                    act()
                else:
                    pl.when(when)(act)
        if stage:
            copies = [
                pltpu.make_async_copy(source, target, sems.at[len(moves) + at])
                for at, (source, target) in enumerate(zip(held, outs))
            ]
            for copy in copies:
                copy.start()
            for copy in copies:
                copy.wait()

    scratch = [pltpu.VMEM(shape.shape, shape.dtype) for shape in out_shapes] if stage else []
    return pl.pallas_call(
        body,
        out_shape=out_shapes,
        in_specs=[pl.BlockSpec(memory_space=pltpu.SMEM)] + [pl.BlockSpec(memory_space=pl.ANY)] * count,
        out_specs=[pl.BlockSpec(memory_space=pl.ANY if stage else pltpu.VMEM)] * out_count,
        scratch_shapes=[pltpu.SemaphoreType.DMA((SEMAPHORES,))] + scratch,
        compiler_params=pltpu.CompilerParams(vmem_limit_bytes=62 * 1024 * 1024),
        name=name,
    )(jnp.zeros(5, jnp.int32) if place is None else place.spot, *inputs)


class Pipe:
    def __init__(self, steps):
        self.steps, self.value = steps, None
        self.feed(None)

    def feed(self, results):
        try:
            self.wants = self.steps.send(results)
        except StopIteration as stop:
            self.wants, self.value = None, stop.value


def prepared(pipe):
    return (lambda *values: values), tuple(value for _, value in pipe.wants)


def prepare(pipe, values):
    pipe.wants = [(hop, value) for (hop, _), value in zip(pipe.wants, values)]


class Clock:
    def __init__(self):
        self.fence = ()

    def behind(self, values):
        return lax.optimization_barrier((values, self.fence))[0]

    def slot(self, pipes, *works, loose=()):
        pipes = [pipe for pipe in (*pipes, *loose) if pipe.wants]
        asked = [self.behind([value for _, value in pipe.wants]) for pipe in pipes]
        given = [lax.optimization_barrier((inputs, self.fence, asked))[0] for _, inputs in works]
        results = [work(*inputs) for (work, _), inputs in zip(works, given)]
        got = [[hop(value) for (hop, _), value in zip(pipe.wants, values)] for pipe, values in zip(pipes, asked)]
        self.fence = ([values for pipe, values in zip(pipes, got) if pipe not in loose], results)
        first = ()
        for pipe, values in zip(pipes, got):
            pipe.feed(lax.optimization_barrier((values, first))[0])
            first = [value for _, value in pipe.wants] if pipe.wants else first
        return results[0] if len(results) == 1 else results


def line_gather(place, piece):
    got = yield [(place.swap_z(turn), piece) for turn in range(1, place.depth)]
    return jnp.stack([piece, *got])


def spread_to(place, values, outs, at):
    count, shape = len(values), values[0].shape[1:]
    two = jax.ShapeDtypeStruct((2, count, *shape), values[0].dtype)

    def cut(spot, ins, outs):
        y = spot[2]
        moves = []
        for k, ref in enumerate(ins):
            for j in range(2):
                moves.append((None, ref.at[2 * y + j], outs[0].at[j, k]))
                moves.append((None, ref.at[2 - 2 * y + j], outs[1].at[j, k]))
        return moves

    own, send = run_moves("spread_cut", place, values, [two, two], cut)
    (far,) = yield [(place.swap_y, send)]

    def pick(spot, ins, outs):
        return [(None, ref.at[1 - spot[3]], outs[0].at[k]) for k, ref in enumerate(ins)]

    (send,) = run_moves("spread_pick", place, [own, far], [two], pick)
    (other,) = yield [(place.swap_c, send)]

    def put(spot, ins, outs):
        mine, n = spot[3], spot[4]
        moves = []
        for k in range(count):
            sources = (ins[0].at[mine, k], ins[2].at[0, k], ins[1].at[mine, k], ins[2].at[1, k])
            moves += [(None, ref, outs[k].at[at(n ^ turn)]) for turn, ref in enumerate(sources)]
        return moves

    out = [jax.ShapeDtypeStruct(shape, values[0].dtype) for shape in outs]
    return run_moves("spread_to", place, [own, far, other], out, put)


def plane_gather(place, first, second):
    first_got, second_got = yield [(place.swap_x, first), (place.swap_y, second)]
    first = jnp.stack([first, first_got])
    second = jnp.stack([second, second_got])
    first_far, second_far, first_core, second_core = yield [
        (place.swap_y, first),
        (place.swap_x, second),
        (place.swap_c, first),
        (place.swap_c, second),
    ]
    far_core = yield [(place.swap_c, first_far), (place.swap_c, second_far)]
    return first, first_far, second, second_far, first_core, far_core[0], second_core, far_core[1]


def total(*terms):
    return sum(term.astype(jnp.float32) for term in terms)


HEAD_DIM = 72
STEP = 10
EPS_NORM = 1e-05
BETA_ONE = 0.5
BETA_TWO = 0.5
EPS_ADAM = 1e-06
DECAY = 0.01
RATE = 0.5
RATE_TABLE = 0.1
NEGATIVE = -1e30
BOTH = ("wide", "narrow")
TABLE_COLS = 128


def project(left, right):
    return jnp.dot(left, right, preferred_element_type=jnp.float32)


def across(left, right):
    return lax.dot_general(
        left, right, (((0,), (0,)), ((), ())), preferred_element_type=jnp.float32
    )


def against(left, right):
    return lax.dot_general(
        left, right, (((1,), (1,)), ((), ())), preferred_element_type=jnp.float32
    )


def adam_step(grad, moment, square):
    new_mom = BETA_ONE * moment + (1.0 - BETA_ONE) * grad
    new_sq = BETA_TWO * square + (1.0 - BETA_TWO) * grad * grad
    step_dir = (
        new_mom / (1.0 - BETA_ONE**STEP) / (jnp.sqrt(new_sq / (1.0 - BETA_TWO**STEP)) + EPS_ADAM)
    )
    return (new_mom, new_sq, step_dir)


ATTN_VMEM = 60 * 1024 * 1024


def head_window(head):
    start = head * HEAD_DIM
    base = start // 128 * 128
    width = 128 if start - base + HEAD_DIM <= 128 else 256
    return base, width, start - base


def lane_mask(rows, width, offset):
    lane = lax.broadcasted_iota(jnp.int32, (rows, width), 1)
    return (lane >= offset) & (lane < offset + HEAD_DIM)


def score_rows(queries, keys, length, slots):
    logits = against(keys, queries) * (1.0 / math.sqrt(HEAD_DIM))
    key_at = lax.broadcasted_iota(jnp.int32, (slots, slots), 0)
    return jnp.where(key_at < length, logits, NEGATIVE)


def put_rows(ref, window, mask, value):
    ref[:, window] = jnp.where(mask, value, ref[:, window])


def attend_kernel(model, lengths_ref, qkv_ref, out_ref, lse_ref):
    slots = qkv_ref.shape[0]
    length = lengths_ref[pl.program_id(0)]
    for head in range(model // HEAD_DIM):
        base, width, offset = head_window(head)
        mask = lane_mask(slots, width, offset)
        window = pl.ds(base, width)
        queries = jnp.where(mask, qkv_ref[:, window], jnp.zeros((), LOW))
        logits = score_rows(queries, qkv_ref[:, pl.ds(model + base, width)], length, slots)
        top = jnp.max(logits, 0, keepdims=True)
        expo = jnp.exp(logits - top)
        scale = jnp.sum(expo, 0, keepdims=True)
        probs = (expo * (1.0 / scale)).astype(LOW)
        lse_ref[0, pl.ds(head, 1), :] = top + jnp.log(scale)
        heads_out = across(probs, qkv_ref[:, pl.ds(2 * model + base, width)]).astype(LOW)
        put_rows(out_ref, window, mask, heads_out)


def attend_back_kernel(model, lengths_ref, qkv_ref, d_heads_ref, lse_ref, out_ref):
    slots = qkv_ref.shape[0]
    length = lengths_ref[pl.program_id(0)]
    scale = 1.0 / math.sqrt(HEAD_DIM)
    for head in range(model // HEAD_DIM):
        base, width, offset = head_window(head)
        mask = lane_mask(slots, width, offset)
        window = pl.ds(base, width)
        key_window = pl.ds(model + base, width)
        value_window = pl.ds(2 * model + base, width)
        zero = jnp.zeros((), LOW)
        queries = jnp.where(mask, qkv_ref[:, window], zero)
        d_heads = jnp.where(mask, d_heads_ref[:, window], zero)
        keys = qkv_ref[:, key_window]
        logits = score_rows(queries, keys, length, slots)
        probs = jnp.exp(logits - lse_ref[0, pl.ds(head, 1), :])
        d_probs = against(qkv_ref[:, value_window], d_heads)
        weighted = probs * d_probs
        d_logits = (weighted - probs * jnp.sum(weighted, 0, keepdims=True)).astype(LOW)
        d_queries = (across(d_logits, keys) * scale).astype(LOW)
        d_keys = (project(d_logits, queries) * scale).astype(LOW)
        d_values = project(probs.astype(LOW), d_heads).astype(LOW)
        put_rows(out_ref, window, mask, d_queries)
        put_rows(out_ref, key_window, mask, d_keys)
        put_rows(out_ref, value_window, mask, d_values)


def item_block(slots, cols):
    return pl.BlockSpec((slots, cols), lambda i: (i, 0))


def lse_block(heads, slots):
    return pl.BlockSpec((1, heads, slots), lambda i: (i, 0, 0))


def attend(lengths, qkv, model):
    items = lengths.shape[0]
    slots = qkv.shape[0] // items
    heads = model // HEAD_DIM
    return pl.pallas_call(
        functools.partial(attend_kernel, model),
        grid=(items,),
        out_shape=[
            jax.ShapeDtypeStruct((items * slots, model), LOW),
            jax.ShapeDtypeStruct((items, heads, slots), jnp.float32),
        ],
        in_specs=[pl.BlockSpec(memory_space=pltpu.SMEM), item_block(slots, 3 * model)],
        out_specs=[item_block(slots, model), lse_block(heads, slots)],
        compiler_params=pltpu.CompilerParams(vmem_limit_bytes=ATTN_VMEM),
        name="attend",
    )(lengths, qkv)


def attend_back(lengths, qkv, d_heads, lse, model):
    items = lengths.shape[0]
    slots = qkv.shape[0] // items
    heads = model // HEAD_DIM
    return pl.pallas_call(
        functools.partial(attend_back_kernel, model),
        grid=(items,),
        out_shape=jax.ShapeDtypeStruct((items * slots, 3 * model), LOW),
        in_specs=[
            pl.BlockSpec(memory_space=pltpu.SMEM),
            item_block(slots, 3 * model),
            item_block(slots, model),
            lse_block(heads, slots),
        ],
        out_specs=item_block(slots, 3 * model),
        compiler_params=pltpu.CompilerParams(vmem_limit_bytes=ATTN_VMEM),
        name="attend_back",
    )(lengths, qkv, d_heads, lse)


KERNEL_VMEM = 60 * 1024 * 1024


def whole(shape):
    return pl.BlockSpec(shape, lambda *_: (0,) * len(shape))


def call(body, name, grid, ins, outs, scratch=(), scalars=()):
    spec = pltpu.PrefetchScalarGridSpec(
        num_scalar_prefetch=len(scalars),
        grid=grid,
        in_specs=[block for _, block in ins],
        out_specs=[block for _, _, block in outs],
        scratch_shapes=list(scratch),
    )
    return pl.pallas_call(
        body,
        grid_spec=spec,
        out_shape=[jax.ShapeDtypeStruct(shape, dtype) for shape, dtype, _ in outs],
        compiler_params=pltpu.CompilerParams(vmem_limit_bytes=KERNEL_VMEM),
        name=name,
    )(*scalars, *[array for array, _ in ins])


def gelu_pair(value):
    scale = math.sqrt(2.0 / math.pi)
    square = value * value
    bend = jnp.tanh(scale * value * (1.0 + 0.044715 * square))
    half = 0.5 * (1.0 + bend)
    slope = half + 0.5 * value * (1.0 - bend * bend) * (scale * (1.0 + 3.0 * 0.044715 * square))
    return value * half, slope


def widen_kernel(act_ref, weight_ref, hidden_ref, slope_ref):
    value, slope = gelu_pair(project(act_ref[...], weight_ref[...]))
    hidden_ref[...] = value.astype(LOW)
    slope_ref[...] = slope.astype(LOW)


def widen_rows(act, weight, block=768):
    rows, model = act.shape
    cols = weight.shape[1]
    tile = pl.BlockSpec((rows, block), lambda j: (0, j))
    return call(
        widen_kernel,
        "widen",
        (cols // block,),
        [(act, whole((rows, model))), (weight, pl.BlockSpec((model, block), lambda j: (0, j)))],
        [((rows, cols), LOW, tile), ((rows, cols), LOW, tile)],
    )


def flat(ref):
    return ref[...].reshape(-1, ref.shape[-1])


def fc2_block(weight, block):
    each = weight.shape[1]
    return pl.BlockSpec((block // each, each, weight.shape[2]), lambda k: (k, 0, 0))


def narrow_back_kernel(grad_ref, weight_ref, slope_ref, out_ref):
    out_ref[...] = (against(grad_ref[...], flat(weight_ref)) * slope_ref[...]).astype(LOW)


def narrow_back_rows(grad, weight, slope, block=1152):
    rows, model = grad.shape
    cols = slope.shape[1]
    tile = pl.BlockSpec((rows, block), lambda j: (0, j))
    (out,) = call(
        narrow_back_kernel,
        "narrow_back",
        (cols // block,),
        [(grad, whole((rows, model))), (weight, fc2_block(weight, block)), (slope, tile)],
        [((rows, cols), LOW, tile)],
    )
    return out


def narrow_kernel(hidden_ref, weight_ref, second_ref, out_ref, total_ref):
    step = pl.program_id(0)

    @pl.when(step == 0)
    def _():
        total_ref[...] = second_ref[...]

    total_ref[...] += project(hidden_ref[...], flat(weight_ref))

    @pl.when(step == pl.num_programs(0) - 1)
    def _():
        out_ref[...] = total_ref[...].astype(LOW)


def narrow_rows(hidden, weight, second, block=1152):
    rows, depth = hidden.shape
    model = second.shape[1]
    (out,) = call(
        narrow_kernel,
        "narrow",
        (depth // block,),
        [
            (hidden, pl.BlockSpec((rows, block), lambda k: (0, k))),
            (weight, fc2_block(weight, block)),
            (second, whole((rows, model))),
        ],
        [((rows, model), LOW, whole((rows, model)))],
        [pltpu.VMEM((rows, model), jnp.float32)],
    )
    return out


def row_grads_kernel(spot_ref, left_ref, right_ref, send_ref, keep_ref, full_ref):
    core = spot_ref[3]
    units, chips, each, _ = send_ref.shape
    full_ref[...] = across(left_ref[...], right_ref[...])
    for chip in range(chips):
        for ref, at in ((send_ref, 1 - core), (keep_ref, core)):
            for unit in range(units):
                start = pl.multiple_of(units * each * (2 * chip + at) + each * unit, 8)
                ref[unit, chip] = full_ref[pl.ds(start, each), :].astype(LOW)


def row_grads(place, left, right, each, block=1152):
    rows, width = left.shape
    cols = right.shape[1]
    chips = block // (4 * each)
    tile = pl.BlockSpec((2, chips, each, cols), lambda k, spot: (0, k, 0, 0))
    shape = (2, width // (4 * each), each, cols)
    return call(
        row_grads_kernel,
        "row_grads",
        (width // block,),
        [(left, pl.BlockSpec((rows, block), lambda k, spot: (0, k))), (right, whole((rows, cols)))],
        [(shape, LOW, tile)] * 2,
        [pltpu.VMEM((block, cols), jnp.float32)],
        [place.spot],
    )


def column_grads_kernel(spot_ref, left_ref, right_ref, send_ref, keep_ref):
    step = pl.program_id(0)
    product = across(left_ref[...], right_ref[...]).astype(LOW)

    @pl.when(step < 2)
    def _():
        send_ref[0] = product

    @pl.when(step >= 2)
    def _():
        keep_ref[0] = product


def column_grads(place, left, right):
    rows, model = left.shape

    def unit(u, spot):
        return (u // 2 + 1 - spot[3]) % 2 * 2 + u % 2

    return call(
        column_grads_kernel,
        "column_grads",
        (4,),
        [
            (left, pl.BlockSpec((rows, model), lambda u, spot: (0, 0))),
            (right, pl.BlockSpec((rows, model), lambda u, spot: (0, unit(u, spot)))),
        ],
        [
            ((2, model, model), LOW, pl.BlockSpec((1, model, model), lambda u, spot: (jnp.minimum(u, 1), 0, 0))),
            ((2, model, model), LOW, pl.BlockSpec((1, model, model), lambda u, spot: (jnp.maximum(u - 2, 0), 0, 0))),
        ],
        scalars=[place.spot],
    )


def mixed_grads_kernel(spot_ref, act_ref, heads_ref, right_ref, second_ref, send_ref, keep_ref):
    step = pl.program_id(0)
    last = (step % 2 == 1) & ((step // 2 + 1 - spot_ref[3]) % 2 == 1)

    def put(product):
        product = product.astype(LOW)

        @pl.when(step < 2)
        def _():
            send_ref[0] = product

        @pl.when(step >= 2)
        def _():
            keep_ref[0] = product

    @pl.when(last)
    def _():
        put(across(heads_ref[...], second_ref[...]))

    @pl.when(jnp.logical_not(last))
    def _():
        put(across(act_ref[...], right_ref[...]))


def mixed_grads(place, act, heads_out, d_projected, d_second):
    rows, model = act.shape
    full = pl.BlockSpec((rows, model), lambda u, spot: (0, 0))

    def unit(u, spot):
        return jnp.minimum((u // 2 + 1 - spot[3]) % 2 * 2 + u % 2, 2)

    return call(
        mixed_grads_kernel,
        "mixed_grads",
        (4,),
        [
            (act, full),
            (heads_out, full),
            (d_projected, pl.BlockSpec((rows, model), lambda u, spot: (0, unit(u, spot)))),
            (d_second, full),
        ],
        [
            ((2, model, model), LOW, pl.BlockSpec((1, model, model), lambda u, spot: (jnp.minimum(u, 1), 0, 0))),
            ((2, model, model), LOW, pl.BlockSpec((1, model, model), lambda u, spot: (jnp.maximum(u - 2, 0), 0, 0))),
        ],
        scalars=[place.spot],
    )


def norm_back_sums(d_act, normed, inv, gain):
    scaled = d_act * gain
    back = inv * (
        scaled
        - jnp.mean(scaled, -1, keepdims=True)
        - normed * jnp.mean(scaled * normed, -1, keepdims=True)
    )
    sums = jnp.concatenate(
        [jnp.sum(d_act * normed, 0, keepdims=True), jnp.sum(d_act, 0, keepdims=True)], 0
    )
    return back, sums


def norm_rows(value):
    center = value - jnp.mean(value, -1, keepdims=True)
    inv = lax.rsqrt(jnp.mean(center * center, -1, keepdims=True) + EPS_NORM)
    return center * inv, inv


def widen_back_kernel(d_pre_ref, w_fc1_ref, w_proj_ref, grad_ref, second_ref, table_ref, d_second_ref, low_ref, heads_ref, sums_ref, total_ref):
    step = pl.program_id(0)

    @pl.when(step == 0)
    def _():
        total_ref[...] = jnp.zeros_like(total_ref)

    total_ref[...] += against(d_pre_ref[...], w_fc1_ref[...])

    @pl.when(step == pl.num_programs(0) - 1)
    def _():
        normed, inv = norm_rows(second_ref[...])
        back, sums = norm_back_sums(total_ref[...], normed, inv, table_ref[2:3, :])
        d_second = grad_ref[...].astype(jnp.float32) + back
        low = d_second.astype(LOW)
        sums_ref[...] = sums
        d_second_ref[...] = d_second
        low_ref[...] = low
        heads_ref[...] = against(low, w_proj_ref[...]).astype(LOW)


def widen_back_rows(d_pre, w_fc1, w_proj, grad, second, table, block=1536):
    rows, depth = d_pre.shape
    model = grad.shape[1]
    full = whole((rows, model))
    return call(
        widen_back_kernel,
        "widen_back",
        (depth // block,),
        [
            (d_pre, pl.BlockSpec((rows, block), lambda k: (0, k))),
            (w_fc1, pl.BlockSpec((model, block), lambda k: (0, k))),
            (w_proj, whole((model, model))),
            (grad, full),
            (second, full),
            (table, whole((4, model))),
        ],
        [
            ((rows, model), jnp.float32, full),
            ((rows, model), LOW, full),
            ((rows, model), LOW, full),
            ((2, model), jnp.float32, whole((2, model))),
        ],
        [pltpu.VMEM((rows, model), jnp.float32)],
    )


def enter_back_kernel(d_projected_ref, weight_ref, d_second_ref, first_ref, table_ref, low_ref, sums_ref, total_ref):
    step = pl.program_id(0)

    @pl.when(step == 0)
    def _():
        total_ref[...] = jnp.zeros_like(total_ref)

    total_ref[...] += against(d_projected_ref[...], weight_ref[...])

    @pl.when(step == pl.num_programs(0) - 1)
    def _():
        normed, inv = norm_rows(first_ref[...])
        back, sums = norm_back_sums(total_ref[...], normed, inv, table_ref[0:1, :])
        sums_ref[...] = sums
        low_ref[...] = (d_second_ref[...] + back).astype(LOW)


def enter_back_rows(d_projected, weight, d_second, first, table, block=1152):
    rows, depth = d_projected.shape
    model = first.shape[1]
    full = whole((rows, model))
    return call(
        enter_back_kernel,
        "enter_back",
        (depth // block,),
        [
            (d_projected, pl.BlockSpec((rows, block), lambda k: (0, k))),
            (weight, pl.BlockSpec((model, block), lambda k: (0, k))),
            (d_second, full),
            (first, full),
            (table, whole((4, model))),
        ],
        [((rows, model), LOW, full), ((2, model), jnp.float32, whole((2, model)))],
        [pltpu.VMEM((rows, model), jnp.float32)],
    )


def enter_kernel(token_ref, store_ref, weight_ref, table_ref, first_ref, act_ref):
    model = token_ref.shape[1]
    blocks, items, each, _ = store_ref.shape
    parts = [
        sum(
            across(store_ref[at, item], weight_ref[model + each * at : model + each * (at + 1), :])
            for at in range(blocks)
        )
        for item in range(items)
    ]
    first = project(token_ref[...], weight_ref[:model, :]) + jnp.concatenate(parts, 0)
    first_ref[...] = first
    normed, _ = norm_rows(first)
    act_ref[...] = (normed * table_ref[0:1, :] + table_ref[1:2, :]).astype(LOW)


def enter_rows(token_rows, store, weight, table):
    rows, model = token_rows.shape
    full = whole((rows, model))
    return call(
        enter_kernel,
        "enter",
        (1,),
        [(token_rows, full), (store, whole(store.shape)), (weight, whole((2 * model, model))), (table, whole((4, model)))],
        [((rows, model), jnp.float32, full), ((rows, model), LOW, full)],
    )


def skip_grads_kernel(token_ref, store_ref, right_ref, table_ref, out_ref):
    step = pl.program_id(0)
    cols = right_ref.shape[1]
    out_ref[:, cols:] = table_ref[...].astype(LOW)

    @pl.when(step == 0)
    def _():
        out_ref[:, :cols] = across(token_ref[...], right_ref[...]).astype(LOW)

    @pl.when(step == 1)
    def _():
        blocks, items, block, slots = store_ref.shape
        for at in range(blocks):
            parts = [
                project(store_ref[at, item], right_ref[slots * item : slots * (item + 1), :])
                for item in range(items)
            ]
            out_ref[block * at : block * (at + 1), :cols] = sum(parts).astype(LOW)


def skip_grads_rows(token_rows, store, right, table):
    rows, model = token_rows.shape
    cols = right.shape[1]
    extra = table.shape[1]
    (out,) = call(
        skip_grads_kernel,
        "skip_grads",
        (2,),
        [
            (token_rows, whole((rows, model))),
            (store, whole(store.shape)),
            (right, whole((rows, cols))),
            (table, pl.BlockSpec((model, extra), lambda k: (k, 0))),
        ],
        [((2 * model, cols + extra), LOW, pl.BlockSpec((model, cols + extra), lambda k: (k, 0)))],
    )
    return out


def leave_back_kernel(left_ref, weight_ref, token_ref, store_ref):
    model = left_ref.shape[1]
    blocks, items, each, slots = store_ref.shape
    token_ref[...] = against(left_ref[...], weight_ref[:model, :]).astype(LOW)
    for at in range(blocks):
        rows = weight_ref[model + each * at : model + each * (at + 1), :]
        for item in range(items):
            left = left_ref[slots * item : slots * (item + 1), :]
            store_ref[at, item] = against(rows, left).astype(LOW)


def leave_back_rows(left, weight, blocks, items):
    rows, model = left.shape
    shape = (blocks, items, model // blocks, rows // items)
    return call(
        leave_back_kernel,
        "leave_back",
        (1,),
        [(left, whole((rows, model))), (weight, whole((2 * model, model)))],
        [((rows, model), LOW, whole((rows, model))), (shape, LOW, whole(shape))],
    )


def product_kernel(left_ref, right_ref, out_ref):
    out_ref[...] = project(left_ref[...], right_ref[...]).astype(LOW)


def product_rows(left, right, block=1152):
    rows, depth = left.shape
    cols = right.shape[1]
    (out,) = call(
        product_kernel,
        "product",
        (cols // block,),
        [(left, whole((rows, depth))), (right, pl.BlockSpec((depth, block), lambda j: (0, j)))],
        [((rows, cols), LOW, pl.BlockSpec((rows, block), lambda j: (0, j)))],
    )
    return out


def merge_kernel(heads_ref, weight_ref, first_ref, table_ref, second_ref, act_ref):
    second = first_ref[...] + project(heads_ref[...], weight_ref[...])
    second_ref[...] = second
    normed, _ = norm_rows(second)
    act_ref[...] = (normed * table_ref[2:3, :] + table_ref[3:4, :]).astype(LOW)


def merge_rows(heads_out, weight, first, table):
    rows, model = heads_out.shape
    full = whole((rows, model))
    return call(
        merge_kernel,
        "merge",
        (1,),
        [(heads_out, full), (weight, whole((model, model))), (first, full), (table, whole((4, model)))],
        [((rows, model), jnp.float32, full), ((rows, model), LOW, full)],
    )


def summed(*refs):
    value = refs[0][...].astype(jnp.float32)
    for ref in refs[1:]:
        value += ref[...].astype(jnp.float32).reshape(value.shape)
    return value


def hop_one_kernel(spot_ref, keep_one, got_one, keep_two, got_two, one_ref, two_ref):
    one_ref[...] = summed(keep_one, got_one).reshape(one_ref.shape).astype(LOW)
    two_ref[...] = summed(keep_two, got_two).reshape(two_ref.shape).astype(LOW)


def hop_one(place, keep, got):
    depth, rows, cols = place.depth, *keep.shape[4:]
    block = (1, depth, 1, 1, rows, cols)
    one = pl.BlockSpec(block, lambda j, spot: (0, 0, 1 - spot[1], j, 0, 0))
    two = pl.BlockSpec(block, lambda j, spot: (1, 0, j, 1 - spot[2], 0, 0))
    out = ((depth, 2, rows, cols), LOW, pl.BlockSpec((depth, 1, rows, cols), lambda j, spot: (0, j, 0, 0)))
    ins = [(keep, one), (got, one), (keep, two), (got, two)]
    return call(hop_one_kernel, "hop_one", (2,), ins, [out, out], scalars=[place.spot])


def hop_two_kernel(spot_ref, keep_one, got_one, near_one, keep_two, got_two, near_two, one_ref, two_ref):
    one_ref[...] = summed(keep_one, got_one, near_one).reshape(one_ref.shape).astype(LOW)
    two_ref[...] = summed(keep_two, got_two, near_two).reshape(two_ref.shape).astype(LOW)


def hop_two(place, keep, got, near_one, near_two):
    depth, rows, cols = place.depth, *keep.shape[4:]
    block = (1, depth // 2, 1, 1, rows, cols)
    one = pl.BlockSpec(block, lambda j, spot: (0, j, spot[1], 1 - spot[2], 0, 0))
    two = pl.BlockSpec(block, lambda j, spot: (1, j, 1 - spot[1], spot[2], 0, 0))
    block = (depth // 2, 1, rows, cols)
    ins = [
        (keep, one),
        (got, one),
        (near_one, pl.BlockSpec(block, lambda j, spot: (j, 1 - spot[2], 0, 0))),
        (keep, two),
        (got, two),
        (near_two, pl.BlockSpec(block, lambda j, spot: (j, 1 - spot[1], 0, 0))),
    ]
    out = ((depth, rows, cols), LOW, pl.BlockSpec((depth // 2, rows, cols), lambda j, spot: (j, 0, 0)))
    return call(hop_two_kernel, "hop_two", (2,), ins, [out, out], scalars=[place.spot])


def hop_three_kernel(spot_ref, *refs):
    ins, outs = refs[:8], refs[8:]
    for turn, ref in enumerate(outs):
        at = spot_ref[0] ^ turn
        for unit in range(2):
            keep, got, near, far = ins[4 * unit : 4 * unit + 4]
            parts = keep[0, at, 0, 0], got[0, at, 0, 0], near[at, 0], far[at]
            ref[unit] = total(*parts).astype(ref.dtype)


def hop_three(place, keep, got, near_one, near_two, far_one, far_two):
    depth, rows, cols = place.depth, *keep.shape[4:]
    block = (1, depth, 1, 1, rows, cols)
    near = (depth, 1, rows, cols)
    one = pl.BlockSpec(block, lambda t, spot: (0, 0, spot[1], spot[2], 0, 0))
    two = pl.BlockSpec(block, lambda t, spot: (1, 0, spot[1], spot[2], 0, 0))
    ins = [
        (keep, one),
        (got, one),
        (near_one, pl.BlockSpec(near, lambda t, spot: (0, spot[2], 0, 0))),
        (far_one, whole(far_one.shape)),
        (keep, two),
        (got, two),
        (near_two, pl.BlockSpec(near, lambda t, spot: (0, spot[1], 0, 0))),
        (far_two, whole(far_two.shape)),
    ]
    shape = (2, rows, cols)
    outs = [(shape, jnp.float32 if turn == 0 else LOW, whole(shape)) for turn in range(depth)]
    return call(hop_three_kernel, "hop_three", (1,), ins, outs, scalars=[place.spot])


def halves_by_core(place, both):
    half = both.shape[2] // 2
    mine = lax.dynamic_slice_in_dim(both, place.c * half, half, 2)
    (got,) = yield [(place.swap_c, lax.dynamic_slice_in_dim(both, (1 - place.c) * half, half, 2))]
    first = place.c == 0
    return jnp.concatenate([jnp.where(first, mine, got), jnp.where(first, got, mine)], 1)


def gather_columns(place, block):
    unit = block.shape[1] // 2
    line = yield from line_gather(place, block)
    return (yield from plane_gather(place, line[..., :unit], line[..., unit:]))


def plane_moves(spot, kept, out_one, out_two, when_one=None, when_two=None):
    z, x, y = spot[0], spot[1], spot[2]
    moves = []
    for turn in range(2):
        for line in range(kept[0].shape[1]):
            depth = z ^ line
            at = x ^ turn
            moves.append((when_one, kept[0].at[turn, line], out_one(depth, at, y)))
            moves.append((when_one, kept[1].at[turn, line], out_one(depth, at, 1 - y)))
            at = y ^ turn
            moves.append((when_two, kept[2].at[turn, line], out_two(depth, x, at)))
            moves.append((when_two, kept[3].at[turn, line], out_two(depth, 1 - x, at)))
    return moves


def gather_qkvp(place, block):
    rows, unit = block.shape[0], block.shape[1] // 2
    kept = yield from gather_columns(place, block)
    depth = place.depth
    lead = (depth, CHIP_X, CHIP_Y, rows)
    out = [jax.ShapeDtypeStruct(lead + (3 * unit,), LOW), jax.ShapeDtypeStruct(lead + (unit,), LOW)]

    def plan(spot, ins, outs):
        moves = []
        for core in range(2):
            at = spot[3] if core == 0 else 1 - spot[3]
            start = pl.multiple_of(at * (2 * unit), 128)
            x, y = spot[1], spot[2]

            def one(z, x, y, start=start):
                return outs[0].at[z, x, y, :, pl.ds(start, unit)]

            def key(z, x, y):
                return outs[0].at[z, x, y, :, pl.ds(unit, unit)]

            def last(z, x, y):
                return outs[1].at[z, x, y]

            kept = ins[4 * core : 4 * core + 4]
            for turn, move in enumerate(plane_moves(spot, kept, one, key)):
                if turn % 4 < 2:
                    moves.append(move)
                else:
                    moves.append((at == 0, move[1], move[2]))
            for turn, move in enumerate(plane_moves(spot, kept, one, last)):
                if turn % 4 >= 2:
                    moves.append((at == 1, move[1], move[2]))
        return moves

    qkv, proj = run_moves("assemble_qkvp", place, kept, out, plan, stage=True)
    full = depth * CHIP_X * CHIP_Y * rows
    return qkv.reshape(full, 3 * unit), proj.reshape(full, unit)


def split_fc1(full, start):
    chips, cores, rows, cols = full.shape
    half = cols - start
    out = [jax.ShapeDtypeStruct((chips, rows, cores * half), LOW)]

    def plan(spot, ins, outs):
        return [
            (None, ins[0].at[:, at, :, pl.ds(start, half)], outs[0].at[:, :, pl.ds(at * half, half)])
            for at in range(cores)
        ]

    (joined,) = run_moves("split_fc1", None, [full], out, plan, stage=True)
    return joined.reshape(chips * rows, cores * half)


def scatter_columns(place, got, keep, cuts):
    parts = yield from scatter_units(place, keep, got, cuts)
    return (yield from halves_to_rows(place, parts))


def halves_to_rows(place, parts):
    rows = parts.shape[1] // 2
    keep = lax.dynamic_slice_in_dim(parts, place.c * rows, rows, 1)
    (got,) = yield [(place.swap_c, lax.dynamic_slice_in_dim(parts, (1 - place.c) * rows, rows, 1))]
    left = place.c == 0
    low, high = jnp.where(left, keep, got), jnp.where(left, got, keep)
    return jnp.concatenate([low[0], low[1], high[0], high[1]], 1)


def scatter_units(place, keep, got, cuts=((1, 2, 3),)):
    lead = (2, place.depth, CHIP_X, CHIP_Y)
    terms = [value.reshape(*lead, -1, value.shape[-1]) if value.ndim == 3 else value.reshape(*lead, *value.shape[2:]) for value in (keep, got)]
    first, second = hop_one(place, *terms)
    near = yield [(place.swap_x, first), (place.swap_y, second)]
    first, second = hop_two(place, *terms, *near)
    far = yield [(place.swap_y, first), (place.swap_x, second)]
    own, *sends = hop_three(place, *terms, *near, *far)
    for turns in cuts:
        got = yield [(place.swap_z(turn), sends[turn - 1]) for turn in turns]
        own = total(own, *got)
    return own


def scatter_fc2(place, send, keep):
    (got,) = yield [(place.swap_c, send)]
    parts = yield from scatter_units(place, keep, got)
    return parts.reshape(-1, parts.shape[2])


def gather_plain(low):
    return lax.all_gather(low, BOTH, axis=0, tiled=True)


def scatter_plain(grad):
    return lax.psum_scatter(grad, BOTH, scatter_dimension=0, tiled=True)


def exchange(hop, value):
    (got,) = yield [(hop, value)]
    return got


def local(
    short,
    wide,
    narrow,
    tokens,
    skip_store,
    cotangent,
    lengths,
    w_skip,
    mom_skip,
    sq_skip,
    w_qkv,
    mom_qkv,
    sq_qkv,
    w_proj,
    mom_proj,
    sq_proj,
    w_fc1,
    mom_fc1,
    sq_fc1,
    w_fc2,
    mom_fc2,
    sq_fc2,
    norm_table,
    norm_mom,
    norm_sq,
):
    place = Place(wide, narrow)
    devices = wide * narrow
    masters = (w_skip, w_qkv, w_proj, w_fc1, w_fc2)
    momenta = (mom_skip, mom_qkv, mom_proj, mom_fc1, mom_fc2)
    seconds = (sq_skip, sq_qkv, sq_proj, sq_fc1, sq_fc2)
    model = tokens.shape[-1]

    items, part = tokens.shape[0] // narrow, tokens.shape[1]
    rows = narrow * items * part
    clock = Clock()

    def swap_all(value):
        return lax.all_to_all(value, BOTH, 0, 0, tiled=True)

    def rows_in(value):
        value = value.reshape(narrow, items, part, model)
        shape = (items, narrow, part, model)
        (value,) = yield from spread_to(place, [value], [shape], lambda at: (slice(None), at))
        return value.reshape(rows, model)

    def rows_out(*values):
        values = [value.reshape(items, narrow, part, model).transpose(1, 0, 2, 3) for value in values]
        values = yield from spread_to(place, values, [value.shape for value in values], lambda at: at)
        return [value.reshape(tokens.shape) for value in values]

    def store_in(value):
        (value,) = yield from spread_to(place, [value], [value.shape], lambda at: at)
        return value

    token_pipe = Pipe(rows_in(tokens))
    store_shape = (narrow, items, model // narrow, narrow * part)
    store_pipe = Pipe(store_in(skip_store.swapaxes(1, 2).reshape(store_shape)))
    cot_pipe = Pipe(rows_in(cotangent))
    lengths = lax.dynamic_slice_in_dim(lengths, lax.axis_index("narrow") * items, items)

    low_skip, low_qkv, low_proj, low_fc1, low_fc2 = (matrix.astype(LOW) for matrix in masters)
    pair = jnp.concatenate([low_qkv, low_proj], 1)
    each = norm_table.shape[0]
    beside = jnp.pad(norm_table.astype(LOW), ((0, low_skip.shape[0] - each), (0, TABLE_COLS - 4)))
    low_skip = jnp.concatenate([low_skip, beside], 1)
    start = model + TABLE_COLS
    if short:
        q_pipe = Pipe(exchange(gather_plain, pair))
        full_fc1 = gather_plain(low_fc1)
        full_skip = gather_plain(low_skip)
        clock.slot([q_pipe, token_pipe, store_pipe])
        clock.slot([token_pipe, store_pipe])
    else:
        halves = Pipe(halves_by_core(place, jnp.stack([pair, low_fc1])))
        clock.slot([halves])
        q_pipe = Pipe(gather_qkvp(place, halves.value[0]))
        full_skip = gather_plain(jnp.concatenate([low_skip, halves.value[1]], 1))
        full_fc1 = split_fc1(full_skip.reshape(-1, CORES, low_skip.shape[0], full_skip.shape[1]), start)
        low_fc2, _ = lax.optimization_barrier((low_fc2, halves.value))
        clock.slot([q_pipe, token_pipe, store_pipe])
        clock.slot([q_pipe, token_pipe, store_pipe])
        clock.slot([q_pipe])
    full_fc2 = lax.all_gather(low_fc2, BOTH, axis=0, tiled=False)
    table = full_skip[:, model:start].reshape(devices, -1, TABLE_COLS)[:, :each, :4]
    table = table.reshape(model, 4).astype(jnp.float32).T

    def mix(act, first, weight, table):
        qkv = product_rows(act, weight[0])
        heads_out, lse = attend(lengths, qkv, model)
        return qkv, lse, heads_out, *merge_rows(heads_out, weight[1], first, table)

    token_rows, store = token_pipe.value, store_pipe.value
    clock.slot([q_pipe])
    w_mix = (q_pipe.value[:, : 3 * model], q_pipe.value[:, 3 * model :]) if short else q_pipe.value
    (first, act_one), w_mix = clock.slot(
        [cot_pipe], (enter_rows, (token_rows, store, full_skip, table)), (lambda *weights: weights, w_mix)
    )
    qkv, lse, heads_out, second, act_two = clock.slot([cot_pipe], (mix, (act_one, first, w_mix, table)))
    hidden, slope = clock.slot([], (widen_rows, (act_two, full_fc1)))

    grad_out = cot_pipe.value

    def leave(second, hidden, weight):
        return narrow_rows(hidden, weight, second)

    def fc2_grads(hidden, grad_out):
        if short:
            return (across(hidden, grad_out),) * 2
        return row_grads(place, hidden, grad_out, masters[4].shape[0] // 2)

    def fc1_grads(act, d_pre):
        return (across(act, d_pre),) * 2 if short else column_grads(place, act, d_pre)

    def mix_back(qkv, d_heads, lse):
        return attend_back(lengths, qkv, d_heads, lse, model)

    def qkvp_grads(act, heads_out, d_projected, d_second_low):
        if short:
            return (jnp.concatenate([across(act, d_projected), across(heads_out, d_second_low)], 1),) * 2
        return mixed_grads(place, act, heads_out, d_projected, d_second_low)

    def skip_grads(token_rows, store, d_first_low, sums):
        sums = jnp.concatenate(sums, 0).T.reshape(devices, each, 4)
        sums = jnp.pad(sums, ((0, 0), (0, masters[0].shape[0] - each), (0, TABLE_COLS - 4)))
        return skip_grads_rows(token_rows, store, d_first_low, sums.reshape(-1, TABLE_COLS))

    def leave_back(d_first_low, weight):
        return leave_back_rows(d_first_low, weight, narrow, items)

    def scatter(steps, send, keep, *cut):
        return Pipe(exchange(scatter_plain, send) if short else steps(place, send, keep, *cut))

    def core(send):
        pipe = Pipe(exchange(place.swap_c, send))
        if short:
            pipe.wants, pipe.value = None, send
        return pipe

    send, keep = clock.slot([], (fc2_grads, (hidden, grad_out)))
    g_back = scatter(scatter_fc2, send, keep)
    d_pre = clock.slot([g_back], (narrow_back_rows, (grad_out, full_fc2, slope)))

    def spread_back(d_pre, act, w_fc1, w_proj, grad_out, second, table):
        return fc1_grads(act, d_pre), widen_back_rows(d_pre, w_fc1, w_proj, grad_out, second, table)

    both, (d_second, d_second_low, d_heads, sums_two) = clock.slot(
        [g_back], (spread_back, (d_pre, act_two, full_fc1, w_mix[1], grad_out, second, table))
    )
    f_core = core(both[0])
    d_projected = clock.slot([g_back, f_core], (mix_back, (qkv, d_heads, lse)))
    f_back = scatter(scatter_columns, f_core.value, both[1], ((1, 2, 3),))

    def turn_back(act, heads_out, d_projected, d_second_low, w_qkv, d_second, first, table):
        grads = qkvp_grads(act, heads_out, d_projected, d_second_low)
        return grads, enter_back_rows(d_projected, w_qkv, d_second, first, table)

    (send, keep), (d_first_low, sums_one) = clock.slot(
        [f_back, g_back],
        (turn_back, (act_one, heads_out, d_projected, d_second_low, w_mix[0], d_second, first, table)),
    )
    q_core = core(send)
    skip_grad, (d_tokens, d_store) = clock.slot(
        [q_core, f_back],
        (skip_grads, (token_rows, store, d_first_low, (sums_one, sums_two))),
        (leave_back, (d_first_low, full_skip)),
    )
    q_back = scatter(scatter_columns, q_core.value, keep, ((1, 2, 3),))
    grad_skip_lin = scatter_plain(skip_grad).astype(jnp.float32)
    out_store_pipe = Pipe(store_in(d_store))
    block_rows, sends = clock.slot(
        [q_back, f_back], (leave, (second, hidden, full_fc2)), prepared(out_store_pipe)
    )
    prepare(out_store_pipe, sends)
    out_pipe = Pipe(rows_out(block_rows, d_tokens))
    sends = clock.slot([q_back, out_store_pipe, f_back], prepared(out_pipe))
    prepare(out_pipe, sends)

    def renew(grad, moment, square, master):
        new_mom, new_sq, step_dir = adam_step(grad, moment, square)
        update = step_dir + DECAY * master
        sums = [jnp.sum(jnp.sum(value * value, 0).reshape(-1, 128), 0) for value in (master, update)]
        return new_mom, new_sq, update, *sums

    def state(index):
        return momenta[index], seconds[index], masters[index]

    renewed = {}
    renewed[3], renewed[4] = clock.slot(
        [q_back, out_pipe, out_store_pipe],
        (renew, (f_back.value, *state(3))),
        (renew, (g_back.value, *state(4))),
    )
    clock.slot([q_back, out_pipe])
    (block_out, grad_tokens), grad_skip = out_pipe.value, out_store_pipe.value
    both = q_back.value
    renewed[1] = renew(both[:, : 3 * model], *state(1))
    renewed[2] = renew(both[:, 3 * model :], *state(2))
    renewed[0] = renew(grad_skip_lin[:, :model], *state(0))
    table_grad = grad_skip_lin[:each, model : model + 4]
    grad_skip = grad_skip.reshape(-1, *store_shape[2:]).swapaxes(1, 2)

    renewed = [renewed[index] for index in range(5)]
    update_list = [value[2] for value in renewed]
    squares = jnp.stack([value[index] for index in (3, 4) for value in renewed])
    squares = jnp.broadcast_to(squares[None], (devices, *squares.shape))
    totals = jnp.sqrt(jnp.sum(swap_all(squares), (0, 2)))
    weight_norm, update_norm = totals[:5], totals[5:]
    trust = weight_norm / (update_norm + EPS_ADAM)
    new_weights = [masters[index] - RATE * trust[index] * update_list[index] for index in range(5)]
    table_mom, table_sq, table_step = adam_step(table_grad, norm_mom, norm_sq)
    new_table = norm_table - RATE_TABLE * table_step
    lamb_stats = jnp.stack([weight_norm, update_norm, trust], 0)
    outs = [block_out, grad_tokens, grad_skip]
    for index in range(5):
        outs += [new_weights[index], *renewed[index][:2], new_weights[index].astype(LOW)]
    return (*outs, new_table, table_mom, table_sq, lamb_stats)


def solution(mesh):
    wide, narrow = mesh.shape["wide"], mesh.shape["narrow"]
    short = not (wide == 8 and narrow == 4)
    rows = P("wide", "narrow", None)
    store = P("wide", None, "narrow")
    shard = P(BOTH, None)
    return jax.shard_map(
        functools.partial(local, short, wide, narrow),
        mesh=mesh,
        in_specs=(rows, store, rows, P("wide")) + (shard,) * 18,
        out_specs=(rows, rows, store) + (shard,) * 23 + (P(),),
        check_vma=False,
    )
```
